32 devices in a mesh: lat: 4 (over z), lon: 4 (over y, core), tm: 2 (over x).
Axes of the slice: x: 2, y: 2, z: 4, core: 2. Of those that a mesh axis runs over, the one named last changes fastest.
Arguments:
- class_ids: int32 [1, 32, 512], P(None, 'lat', 'lon'), may hold values from 0 to 7
- coef_table: float32 [8], replicated, may hold values from 0.2 to 2
- land_mask: int32 [1, 32, 512], P(None, 'lat', 'lon'), may hold values 0 or 1
- cross_cov: float32 [3, 3], replicated, may hold values from -0.4 to 2, as said below
- time_metric: float32 [2, 2], replicated, may hold values from -1.2 to 2.2, as said below
- obs_values: float32 [2048, 3, 128], P(('lat', 'lon', 'tm')), may hold values from -6 to 6
- obs_weight: float32 [2048, 128], P(('lat', 'lon', 'tm')), may hold values from 0.3 to 3
- obs_cells: int32 [2048, 128], P(('lat', 'lon', 'tm')), may hold values from 0 to 1023
- obs_count: int32 [2048], P(('lat', 'lon', 'tm')), may hold values from 1 to 128
- block_owner: int32 [2048, 1], P(('lat', 'lon', 'tm')), may hold values from 0 to 15; in each aligned block of 64 rows (0 to 63, 64 to 127, ...) at most 8 rows name the same one
Outputs:
- solution: float32 [2, 3, 1, 32, 512], P('tm', None, None, 'lat', 'lon')
- residual: float32 [2, 3, 1, 32, 512], P('tm', None, None, 'lat', 'lon')
The draws below stay inside these ranges and needn't reach their ends.
Inputs may be any that keep to these rules, and one draw needn't show every extreme that they name: `block_owner`: the blocks of one device name each owner at most 8 times, a bound that some block reaches. `obs_count`: records at or after a block's count are padding. `obs_cells`: a cell of the owner's tile flattened over months, levels, rows and columns in this order. `time_metric`: symmetric positive definite. `cross_cov`: symmetric positive definite.
All inputs are finite; a program needn't handle non-finite values. No bound on the sum of `land_mask` on one device may be relied on, other than what follows from the above.
Results may differ from the reference program's by a relative error of at most 0.0003.
Values sent between devices are 32-bit elements; how exact they have to be, the bound alone decides.
No kernel may reach another device: no remote copies, remote signals or barrier semaphores. Data moves between devices by JAX's collectives and lax.ppermute only.
A program may use at most 64 MiB of HBM per device.

```python
import math
import jax
import jax.numpy as jnp
import numpy as np
from jax import lax

NV = 3
MD = 1
LEV = 1
CLAT = 8
CLON = 128
NCLASS = 8
BLOCKS_DEV = 64
SLOT = 128
ITERS = 2
NLAT = 32
NLON = 512
MONTHS = 2
NOWN = 16
CAP = 8
NCELL = 1024
BLOCKS = 2048
N_LON = 4
N_TM = 2


def draw_time_metric(key, part):
    key_off, key_diag = jax.random.split(jax.random.fold_in(key, 11))
    random_part = jax.random.uniform(key_off, (MONTHS, MONTHS), jnp.float32, -1.0, 1.0)
    symmetric = 0.5 * (random_part + random_part.T) * (1.2 / MONTHS)
    identity = jnp.eye(MONTHS, dtype=jnp.float32)
    diagonal = jax.random.uniform(key_diag, (MONTHS,), jnp.float32, 1.2, 2.2)
    return symmetric * (1.0 - identity) + identity * diagonal[None, :]


def draw_cross_cov(key, part):
    key_off, key_diag = jax.random.split(jax.random.fold_in(key, 23))
    random_part = jax.random.uniform(key_off, (NV, NV), jnp.float32, -0.4, 0.4)
    symmetric = 0.5 * (random_part + random_part.T)
    identity = jnp.eye(NV, dtype=jnp.float32)
    diagonal = jax.random.uniform(key_diag, (NV,), jnp.float32, 1.0, 2.0)
    return symmetric * (1.0 - identity) + identity * diagonal[None, :]


def plant(drawn, rng, low, high):
    longest = drawn.shape.index(max(drawn.shape))
    spots = []
    for shift in (0, 1):
        where = [jax.random.randint(jax.random.fold_in(rng, axis), (), 0, length) for axis, length in enumerate(drawn.shape)]
        where[longest] = (where[longest] + shift) % drawn.shape[longest]
        spots.append(tuple(where))
    return drawn.at[spots[0]].set(low).at[spots[1]].set(high)


def levels(key, dims, shards, low, top_value):
    def one(position, blocks):
        steps = jax.random.uniform(jax.random.fold_in(jax.random.fold_in(key, 6), position), (blocks,), jnp.float32, low / len(shards), top_value / len(shards))
        return jnp.repeat(jnp.exp(steps), dims[position] // blocks).reshape((-1,) + (1,) * (len(dims) - position - 1))

    loudness = one(*shards[0])
    for cut in shards[1:]:
        loudness = loudness * one(*cut)
    return loudness


def shared_out(stream_key, own, number, rows, amount, top, bound, lean):
    order = jax.random.permutation(stream_key, amount)
    heavy_load, ordinary = load_shares(amount, rows * top, bound, lean, True), load_shares(amount, rows * top, bound, lean, False)
    places = jnp.arange(amount)

    def named(lengths, turn):
        used = int((lengths > 0).sum())
        fixed = max(1, used // 4)
        moved = fixed + (places - fixed + turn * (used - fixed)) % max(1, amount - fixed)
        return jnp.zeros((amount,), jnp.int32).at[order[jnp.where(places < fixed, places, moved)]].set(jnp.asarray(lengths, jnp.int32))

    lengths = jnp.where(number % 4 == 0, named(heavy_load, number // 4), named(ordinary, number - number // 4 - 1))
    mixed = jax.random.permutation(jax.random.fold_in(own, 3), amount)
    source_of, sink = mixed[0:amount // 2 * 2:2], mixed[1:amount // 2 * 2:2]
    slack = jnp.minimum(lengths[source_of] - 1, bound - lengths[sink]) // 2
    slack = jnp.where((source_of == order[0]) | (sink == order[0]) | (lengths[sink] == 0), 0, jnp.maximum(slack, 0))
    moved = jax.random.randint(jax.random.fold_in(own, 4), (amount // 2,), 0, 1 << 20) % (slack + 1)
    lengths = lengths.at[source_of].add(-moved).at[sink].add(moved)
    members = jnp.searchsorted(jnp.cumsum(lengths), jnp.arange(rows * top), side="right").astype(jnp.int32)
    grid = members.reshape(top, rows).T
    grid = grid[jax.random.permutation(jax.random.fold_in(own, 1), rows)]
    turn = jax.random.randint(jax.random.fold_in(own, 2), (rows, 1), 0, top)
    return jnp.take_along_axis(grid, (jnp.arange(top)[None, :] + turn) % top, axis=1)


def load_shares(number_of, total, limit, skew, full):
    loads = [(1 << 20) // math.isqrt(grade ** skew) + 1 for grade in range(1, number_of + 1)]
    largest = limit if full else min(limit, max(-(-total // number_of), total * loads[0] // sum(loads)))
    least = 1 if total - largest >= number_of - 1 else 0
    given, rest = [largest] + [least] * (number_of - 1), total - largest - least * (number_of - 1)
    while rest > 0:
        candidates = [i for i in range(1, number_of) if given[i] < largest] or [i for i in range(1, number_of) if given[i] < limit]
        mass, remaining = sum([loads[i] for i in candidates]), rest
        for i in candidates:
            addition = min(limit - given[i], max(1, remaining * loads[i] // mass), rest)
            given[i] = given[i] + addition
            rest = rest - addition
    return np.array(given)


def scatter_about(own_key, shape, scale, bound, cuts=(), kind=jnp.bfloat16):
    entries = jax.random.normal(own_key, shape, jnp.float32) * scale
    if len(cuts) > 0:
        entries = levels(own_key, shape, cuts, -0.22, 0.18) * entries
    return jnp.clip(entries, min=-bound, max=bound).astype(kind)


def setup_inputs(seed: int = 0) -> dict:
    key_of = jax.random.split(jax.random.key(seed), 11)
    class_ids = plant(jax.random.randint(key_of[0], (LEV, NLAT, NLON), 0, NCLASS), jax.random.fold_in(key_of[0], 1), 0, NCLASS - 1).astype(jnp.int32)
    coef_table = jnp.clip(jnp.exp(jax.random.uniform(key_of[1], (NCLASS,), jnp.float32, math.log(0.2), math.log(2.0))), 0.2, 2.0)
    land_mask = plant((jax.random.randint(key_of[2], (LEV, NLAT, NLON), 0, 4) < 3).astype(jnp.int32), jax.random.fold_in(key_of[2], 1), 0, 1)
    cross_cov = draw_cross_cov(jax.random.fold_in(key_of[10], 71), 0)
    time_metric = draw_time_metric(jax.random.fold_in(key_of[10], 71), 0)
    obs_values = scatter_about(key_of[5], (BLOCKS, NV, SLOT), 1.0, 6.0, ((0, 32),), jnp.float32)
    obs_weight = jnp.clip(jnp.exp(math.log(3.0) - 2.3025851 * jax.random.uniform(key_of[6], (BLOCKS, SLOT), jnp.float32) ** levels(key_of[6], (BLOCKS, SLOT), ((0, 32),), -0.2, 0.2)), 0.3, 3.0)
    obs_cells = plant(jax.random.randint(key_of[7], (BLOCKS, SLOT), 0, NCELL), jax.random.fold_in(key_of[7], 1), 0, NCELL - 1).astype(jnp.int32)
    obs_count = plant(jax.random.randint(key_of[8], (BLOCKS,), 1, SLOT + 1), jax.random.fold_in(key_of[8], 1), 1, SLOT).astype(jnp.int32)
    block_owner_keys = jax.random.split(jax.random.fold_in(key_of[9], 1), BLOCKS // BLOCKS_DEV)
    block_owner_turns = jax.random.permutation(jax.random.fold_in(key_of[9], 3), BLOCKS // BLOCKS_DEV)
    block_owner = jax.vmap(lambda own, number: shared_out(jax.random.fold_in(key_of[9], 2), own, number, BLOCKS_DEV, NOWN, 1, CAP, 2))(block_owner_keys, block_owner_turns).reshape((BLOCKS, 1))
    return dict(class_ids=class_ids, coef_table=coef_table, land_mask=land_mask, cross_cov=cross_cov, time_metric=time_metric, obs_values=obs_values, obs_weight=obs_weight, obs_cells=obs_cells, obs_count=obs_count, block_owner=block_owner)


HIGHEST = lax.Precision.HIGHEST


def coefficients(class_ids, coef_table):
    classes = jnp.arange(coef_table.shape[0], dtype=jnp.int32)
    chosen = jnp.where(class_ids[None] == classes[:, None, None, None], coef_table[:, None, None, None], jnp.zeros((), coef_table.dtype))
    return jnp.sum(chosen, axis=0)


def vertical_terms(masked):
    diff_lev = masked[:, :, 1:] - masked[:, :, :-1]
    zero_layer = jnp.zeros_like(masked[:, :, :1])
    return jnp.concatenate([diff_lev, zero_layer], axis=2) - jnp.concatenate([zero_layer, diff_lev], axis=2)


def reference(class_ids, coef_table, land_mask, cross_cov, time_metric, obs_values, obs_weight, obs_cells, obs_count, block_owner):
    diffusivity = coefficients(class_ids, coef_table)
    padded_coef = jnp.pad(diffusivity, ((0, 0), (1, 1), (0, 0)))
    face_lat = 0.5 * (padded_coef[:, :-1] + padded_coef[:, 1:])
    wrapped_coef = jnp.concatenate([diffusivity[..., -1:], diffusivity, diffusivity[..., :1]], axis=-1)
    face_lon = 0.5 * (wrapped_coef[..., :-1] + wrapped_coef[..., 1:])
    sea_mask = land_mask.astype(obs_weight.dtype)[None, None]

    block_index = jnp.arange(BLOCKS, dtype=jnp.int32)
    month_group = (block_index // BLOCKS_DEV) % N_TM
    owner_ids = block_owner[:, 0]
    owner_row = owner_ids // N_LON
    owner_col = owner_ids % N_LON
    month_local = obs_cells // (LEV * CLAT * CLON)
    level_local = (obs_cells // (CLAT * CLON)) % LEV
    row_local = (obs_cells // CLON) % CLAT
    col_local = obs_cells % CLON
    month_global = month_group[:, None] * MD + month_local
    row_global = owner_row[:, None] * CLAT + row_local
    col_global = owner_col[:, None] * CLON + col_local
    global_cell = (((month_global * LEV + level_local) * NLAT + row_global) * NLON + col_global).astype(jnp.int32).reshape(-1)
    slot_index = jnp.arange(SLOT, dtype=jnp.int32)
    live_mask = slot_index[None, :] < obs_count[:, None]
    live_weight = jnp.where(live_mask, obs_weight, jnp.zeros((), obs_weight.dtype))
    total_cells = MONTHS * LEV * NLAT * NLON
    weight_cells = jnp.zeros((total_cells,), obs_weight.dtype).at[global_cell].add(live_weight.reshape(-1))
    weighted = (obs_values * live_weight[:, None, :]).transpose(1, 0, 2).reshape(NV, -1)
    rhs_cells = jnp.zeros((NV, total_cells), obs_weight.dtype).at[:, global_cell].add(weighted)
    right_side = rhs_cells.reshape(NV, MONTHS, LEV, NLAT, NLON).transpose(1, 0, 2, 3, 4) * sea_mask
    obs_diag = weight_cells.reshape(MONTHS, 1, LEV, NLAT, NLON)

    def operate(field):
        masked = field * sea_mask
        padded_lat = jnp.pad(masked, ((0, 0), (0, 0), (0, 0), (1, 1), (0, 0)))
        flux_lat = face_lat * (padded_lat[:, :, :, 1:] - padded_lat[:, :, :, :-1])
        wrapped = jnp.concatenate([masked[..., -1:], masked, masked[..., :1]], axis=-1)
        flux_lon = face_lon * (wrapped[..., 1:] - wrapped[..., :-1])
        spatial = flux_lat[:, :, :, 1:] - flux_lat[:, :, :, :-1] + flux_lon[..., 1:] - flux_lon[..., :-1] + vertical_terms(masked)
        mixed_vars = jnp.einsum("vw,mwlij->mvlij", cross_cov, masked, precision=HIGHEST)
        time_term = jnp.tensordot(time_metric, masked, axes=(1, 0), precision=HIGHEST)
        combined = mixed_vars + time_term - spatial + obs_diag * masked
        return sea_mask * combined + (1.0 - sea_mask) * field

    solution = jnp.zeros_like(right_side)
    residual = right_side
    direction = right_side
    norm_now = jnp.sum(residual * residual)
    for iteration in range(ITERS):
        image_field = operate(direction)
        step_size = norm_now / jnp.sum(direction * image_field)
        solution = solution + step_size * direction
        residual = residual - step_size * image_field
        norm_next = jnp.sum(residual * residual)
        direction = residual + (norm_next / norm_now) * direction
        norm_now = norm_next
    return solution, residual
```

```python
import functools

import jax
import jax.numpy as jnp
from jax import lax
from jax.experimental import pallas as pl
from jax.experimental.pallas import tpu as pltpu
from jax.sharding import PartitionSpec as P

ITERS = 2
GROUP = 8
SPACE = ("lat", "lon")
ALL = ("lat", "lon", "tm")


def tile_kernel(owner_ref, count_ref, table_ref, values_ref, weight_ref, cells_ref, class_ref, land_ref, tiles_ref, plane_ref):
    block_total, variables, slots = values_ref.shape
    owners, stats, rows, cols = tiles_ref.shape

    diffusivity = jnp.zeros((rows, cols), jnp.float32)
    for index in range(table_ref.shape[0]):
        diffusivity = jnp.where(class_ref[0] == index, table_ref[index], diffusivity)
    sea = land_ref[0].astype(jnp.float32)
    plane_ref[...] = jnp.where(lax.axis_index("tm") == 0, diffusivity, sea)

    tiles_ref[...] = jnp.zeros_like(tiles_ref)
    lane = lax.broadcasted_iota(jnp.int32, (1, slots), 1)
    row_ids = lax.broadcasted_iota(jnp.int32, (rows, slots), 0)
    col_ids = lax.broadcasted_iota(jnp.int32, (cols, slots), 0)

    def block_sum(block):
        live = jnp.where(lane < count_ref[block], weight_ref[pl.ds(block, 1), :], 0.0)
        cells = cells_ref[pl.ds(block, 1), :]
        row_hit = row_ids == cells // cols
        terms = [live] + [live * values_ref[block, pl.ds(v, 1), :] for v in range(variables)]
        spread = jnp.concatenate([jnp.where(row_hit, term, 0.0) for term in terms], axis=0)
        high = spread.astype(jnp.bfloat16)
        low = (spread - high.astype(jnp.float32)).astype(jnp.bfloat16)
        col_hot = jnp.where(col_ids == cells % cols, 1.0, 0.0).astype(jnp.bfloat16)
        both = lax.dot_general(
            jnp.concatenate([high, low], axis=0),
            col_hot,
            (((1,), (1,)), ((), ())),
            preferred_element_type=jnp.float32,
        )
        return (both[: stats * rows] + both[stats * rows :]).reshape(stats, rows, cols)

    def step(group, carry):
        sums = [block_sum(group * GROUP + k) for k in range(GROUP)]
        for k in range(GROUP):
            owner = owner_ref[group * GROUP + k]
            tiles_ref[owner] += sums[k]
        return carry

    lax.fori_loop(0, block_total // GROUP, step, 0)


def total(x):
    return jnp.sum(jnp.sum(x, axis=1, keepdims=True), axis=0, keepdims=True)


def descent_kernel(counts, cov_ref, metric_ref, gathered_ref, solution_ref, residual_ref, right, image, direction, diag, coef):
    n_lat, n_lon, n_tm = counts
    rows, cols = gathered_ref.shape[2:]
    height, width = n_lat * rows, n_lon * cols
    variables = right.shape[1]

    def source(i, j, t):
        return (i * n_lon + j) * n_tm + t

    for i in range(n_lat):
        for j in range(n_lon):
            at = (slice(i * rows, (i + 1) * rows), slice(j * cols, (j + 1) * cols))
            coef[(0, *at)] = gathered_ref[source(i, j, 0), variables + 1]
            sea = gathered_ref[source(i, j, 1), variables + 1]
            coef[(1, *at)] = sea
            for t in range(n_tm):
                diag[(t, *at)] = gathered_ref[source(i, j, t), 0]
                for v in range(variables):
                    right[(t, v, *at)] = gathered_ref[source(i, j, t), v + 1] * sea

    def moved(x, dim, forward):
        return pltpu.roll(x, 1 if forward else x.shape[dim] - 1, dim)

    diffusivity, sea = coef[0], coef[1]
    row_ids = lax.broadcasted_iota(jnp.int32, (height, width), 0)
    north_open, south_open = row_ids > 0, row_ids < height - 1
    north = 0.5 * (jnp.where(north_open, moved(diffusivity, 0, True), 0.0) + diffusivity)
    south = 0.5 * (diffusivity + jnp.where(south_open, moved(diffusivity, 0, False), 0.0))
    west = 0.5 * (moved(diffusivity, 1, True) + diffusivity)
    east = 0.5 * (diffusivity + moved(diffusivity, 1, False))
    coef[2] = jnp.where(north_open, north, 0.0)
    coef[3] = jnp.where(south_open, south, 0.0)
    coef[4] = west
    coef[5] = east
    coef[6] = north + south + west + east

    def apply(field):
        along = jnp.zeros((height, width), jnp.float32)
        sea = coef[1]
        for t in range(n_tm):
            masked = [[field[s, v] * sea for v in range(variables)] for s in range(n_tm)]
            centre = diag[t] + coef[6]
            for v in range(variables):
                here = masked[t][v]
                mixed = centre * here
                for w in range(variables):
                    mixed = mixed + cov_ref[v, w] * masked[t][w]
                for s in range(n_tm):
                    mixed = mixed + metric_ref[t, s] * masked[s][v]
                spread = (
                    coef[2] * moved(here, 0, True)
                    + coef[3] * moved(here, 0, False)
                    + coef[4] * moved(here, 1, True)
                    + coef[5] * moved(here, 1, False)
                )
                full = field[t, v]
                result = sea * (mixed - spread) + (1.0 - sea) * full
                image[t, v] = result
                along = along + full * result
        return total(along)

    fields = [(t, v) for t in range(n_tm) for v in range(variables)]
    lat, lon, tm = lax.axis_index("lat"), lax.axis_index("lon"), lax.axis_index("tm")
    own = (pl.ds(pl.multiple_of(lat * rows, rows), rows), pl.ds(pl.multiple_of(lon * cols, cols), cols))

    squares = jnp.zeros((height, width), jnp.float32)
    for t, v in fields:
        squares = squares + right[t, v] * right[t, v]
    norm_now = total(squares)
    for v in range(variables):
        solution_ref[0, v, 0] = jnp.zeros((rows, cols), jnp.float32)
    current = right
    for iteration in range(ITERS):
        step_size = norm_now / apply(current)
        for v in range(variables):
            solution_ref[0, v, 0] += step_size * current[(tm, v, *own)]
        if iteration == ITERS - 1:
            for v in range(variables):
                residual_ref[0, v, 0] = right[(tm, v, *own)] - step_size * image[(tm, v, *own)]
            break
        squares = jnp.zeros((height, width), jnp.float32)
        for t, v in fields:
            after = right[t, v] - step_size * image[t, v]
            image[t, v] = after
            squares = squares + after * after
        norm_next = total(squares)
        share = norm_next / norm_now
        for t, v in fields:
            direction[t, v] = image[t, v] + share * current[t, v]
            right[t, v] = image[t, v]
        norm_now = norm_next
        current = direction


def whole(shape_of):
    return pl.BlockSpec(memory_space=shape_of)


def per_device(class_ids, coef_table, land_mask, cross_cov, time_metric, obs_values, obs_weight, obs_cells, obs_count, block_owner):
    counts = tuple(lax.axis_size(axis) for axis in ALL)
    n_lat, n_lon, n_tm = counts
    rows, cols = class_ids.shape[1:]
    variables = obs_values.shape[1]
    owners = n_lat * n_lon
    vmem, smem = whole(pltpu.VMEM), whole(pltpu.SMEM)
    tiles, plane = pl.pallas_call(
        tile_kernel,
        out_shape=(
            jax.ShapeDtypeStruct((owners, variables + 1, rows, cols), jnp.float32),
            jax.ShapeDtypeStruct((rows, cols), jnp.float32),
        ),
        in_specs=[smem, smem, smem] + [vmem] * 5,
        out_specs=(vmem, vmem),
        compiler_params=pltpu.CompilerParams(vmem_limit_bytes=32 * 1024 * 1024),
    )(block_owner[:, 0], obs_count, coef_table, obs_values, obs_weight, obs_cells, class_ids, land_mask)
    parts = lax.all_to_all(tiles, SPACE, split_axis=0, concat_axis=0, tiled=True)
    mine = jnp.concatenate([jnp.sum(parts, axis=0), plane[None]], axis=0)
    spread = jnp.broadcast_to(mine[None], (owners * n_tm, *mine.shape))
    gathered = lax.all_to_all(spread, ALL, split_axis=0, concat_axis=0, tiled=True)
    height, width = n_lat * rows, n_lon * cols
    field = (n_tm, variables, height, width)
    out = jax.ShapeDtypeStruct((1, variables, 1, rows, cols), jnp.float32)
    return pl.pallas_call(
        functools.partial(descent_kernel, counts),
        out_shape=(out, out),
        in_specs=[smem, smem, vmem],
        out_specs=(vmem, vmem),
        scratch_shapes=[
            pltpu.VMEM(field, jnp.float32),
            pltpu.VMEM(field, jnp.float32),
            pltpu.VMEM(field, jnp.float32),
            pltpu.VMEM((n_tm, height, width), jnp.float32),
            pltpu.VMEM((7, height, width), jnp.float32),
        ],
        compiler_params=pltpu.CompilerParams(vmem_limit_bytes=48 * 1024 * 1024),
    )(cross_cov, time_metric, gathered)


def solution(mesh):
    in_specs = (
        P(None, "lat", "lon"),
        P(),
        P(None, "lat", "lon"),
        P(),
        P(),
        P(ALL, None, None),
        P(ALL, None),
        P(ALL, None),
        P(ALL),
        P(ALL, None),
    )
    out_specs = (P("tm", None, None, "lat", "lon"), P("tm", None, None, "lat", "lon"))
    return jax.shard_map(per_device, mesh=mesh, in_specs=in_specs, out_specs=out_specs, check_vma=False)
```

```python
import functools

import jax
import jax.numpy as jnp
from jax import lax
from jax.experimental import pallas as pl
from jax.experimental.pallas import tpu as pltpu
from jax.sharding import PartitionSpec as P

ITERS = 2
GROUP = 8
INPUTS = 8
ALL = ("lat", "lon", "tm")


def tile_kernel(*refs):
    arguments, (keep_ref, send_ref, planes_ref, tiles) = refs[:INPUTS], refs[INPUTS : INPUTS + 4]
    local, arrived = refs[INPUTS + 4 : -1], refs[-1]
    owner_ref, count_ref, table_ref, values_ref, weight_ref, cells_ref, class_ref, land_ref = local
    copies = [pltpu.make_async_copy(a, b, arrived.at[k]) for k, (a, b) in enumerate(zip(arguments, local))]
    for copy in copies:
        copy.start()
    tiles[...] = jnp.zeros_like(tiles)
    planes_ref[...] = jnp.zeros_like(planes_ref)
    variables, block_total, slots = values_ref.shape
    n_lon, n_lat, stats, rows, cols = tiles.shape
    lat, lon, tm = lax.axis_index("lat"), lax.axis_index("lon"), lax.axis_index("tm")
    for copy in copies:
        copy.wait()

    diffusivity = jnp.zeros((rows, cols), jnp.float32)
    for index in range(table_ref.shape[0]):
        diffusivity = jnp.where(class_ref[0] == index, table_ref[index], diffusivity)
    sea = land_ref[0].astype(jnp.float32)
    planes_ref[0, lat] = jnp.where(tm == 0, diffusivity, sea)

    lane = lax.broadcasted_iota(jnp.int32, (1, slots), 1)
    row_ids = lax.broadcasted_iota(jnp.int32, (rows, slots), 0)
    col_ids = lax.broadcasted_iota(jnp.int32, (cols, slots), 0)

    def block_sum(block):
        live = jnp.where(lane < count_ref[block], weight_ref[pl.ds(block, 1), :], 0.0)
        cells = cells_ref[pl.ds(block, 1), :]
        row_hit = row_ids == cells // cols
        terms = [live] + [live * values_ref[v, pl.ds(block, 1), :] for v in range(variables)]
        spread = jnp.concatenate([jnp.where(row_hit, term, 0.0) for term in terms], axis=0)
        high = spread.astype(jnp.bfloat16)
        low = (spread - high.astype(jnp.float32)).astype(jnp.bfloat16)
        col_hot = jnp.where(col_ids == cells % cols, 1.0, 0.0).astype(jnp.bfloat16)
        both = lax.dot_general(
            jnp.concatenate([high, low], axis=0),
            col_hot,
            (((1,), (1,)), ((), ())),
            preferred_element_type=jnp.float32,
        )
        return (both[: stats * rows] + both[stats * rows :]).reshape(stats, rows, cols)

    def step(group, carry):
        sums = [block_sum(group * GROUP + k) for k in range(GROUP)]
        for k in range(GROUP):
            owner = owner_ref[group * GROUP + k]
            tiles[jnp.bitwise_xor(owner % n_lon, lon), owner // n_lon] += sums[k]
        return carry

    lax.fori_loop(0, block_total // GROUP, step, 0)
    for m in range(n_lon // 2):
        for i in range(n_lat):
            for s in range(stats):
                keep_ref[m, s, i] = tiles[2 * m, i, s]
                send_ref[m, s, i] = tiles[2 * m + 1, i, s]


def total(x):
    return jnp.sum(jnp.sum(x, axis=1, keepdims=True), axis=0, keepdims=True)


def descent_kernel(offsets, cov_ref, metric_ref, near_ref, far_ref, solution_ref, residual_ref, right, image, direction, diag, coef, shared):
    n_lat, rows, cols = near_ref.shape[2:]
    n_tm, variables, height, width = right.shape
    lat, lon, tm = lax.axis_index("lat"), lax.axis_index("lon"), lax.axis_index("tm")

    def place(part_ref, part, lon_offset, tm_offset):
        t = jnp.bitwise_xor(tm, tm_offset)
        across = pl.ds(pl.multiple_of(jnp.bitwise_xor(lon, lon_offset) * cols, cols), cols)
        for i in range(n_lat):
            down = slice(i * rows, (i + 1) * rows)
            diag[t, down, across] = part_ref[part, 0, i]
            for v in range(variables):
                right[t, v, down, across] = part_ref[part, v + 1, i]
            shared[t, down, across] = part_ref[part, variables + 1, i]

    for part, (lon_offset, tm_offset) in enumerate(offsets):
        place(near_ref, part, lon_offset, tm_offset)
        place(far_ref, part, lon_offset + 1, tm_offset)

    def moved(x, dim, forward):
        return pltpu.roll(x, 1 if forward else x.shape[dim] - 1, dim)

    diffusivity, sea = shared[0], shared[1]
    row_ids = lax.broadcasted_iota(jnp.int32, (height, width), 0)
    north_open, south_open = row_ids > 0, row_ids < height - 1
    north = 0.5 * (jnp.where(north_open, moved(diffusivity, 0, True), 0.0) + diffusivity)
    south = 0.5 * (diffusivity + jnp.where(south_open, moved(diffusivity, 0, False), 0.0))
    west = 0.5 * (moved(diffusivity, 1, True) + diffusivity)
    east = 0.5 * (diffusivity + moved(diffusivity, 1, False))
    coef[0] = jnp.where(north_open, north, 0.0)
    coef[1] = jnp.where(south_open, south, 0.0)
    coef[2] = west
    coef[3] = east
    coef[4] = north + south + west + east

    def apply(field):
        along = jnp.zeros((height, width), jnp.float32)
        sea = shared[1]
        for t in range(n_tm):
            masked = [[field[s, v] * sea for v in range(variables)] for s in range(n_tm)]
            centre = diag[t] + coef[4]
            for v in range(variables):
                here = masked[t][v]
                mixed = centre * here
                for w in range(variables):
                    mixed = mixed + cov_ref[v, w] * masked[t][w]
                for s in range(n_tm):
                    mixed = mixed + metric_ref[t, s] * masked[s][v]
                spread = (
                    coef[0] * moved(here, 0, True)
                    + coef[1] * moved(here, 0, False)
                    + coef[2] * moved(here, 1, True)
                    + coef[3] * moved(here, 1, False)
                )
                full = field[t, v]
                result = sea * (mixed - spread) + (1.0 - sea) * full
                image[t, v] = result
                along = along + full * result
        return total(along)

    fields = [(t, v) for t in range(n_tm) for v in range(variables)]
    own = (pl.ds(pl.multiple_of(lat * rows, rows), rows), pl.ds(pl.multiple_of(lon * cols, cols), cols))

    squares = jnp.zeros((height, width), jnp.float32)
    for t, v in fields:
        start = sea * right[t, v]
        right[t, v] = start
        squares = squares + start * start
    norm_now = total(squares)
    for v in range(variables):
        solution_ref[0, v, 0] = jnp.zeros((rows, cols), jnp.float32)
    current = right
    for iteration in range(ITERS):
        step_size = norm_now / apply(current)
        for v in range(variables):
            solution_ref[0, v, 0] += step_size * current[(tm, v, *own)]
        if iteration == ITERS - 1:
            for v in range(variables):
                residual_ref[0, v, 0] = right[(tm, v, *own)] - step_size * image[(tm, v, *own)]
            break
        squares = jnp.zeros((height, width), jnp.float32)
        for t, v in fields:
            after = right[t, v] - step_size * image[t, v]
            image[t, v] = after
            squares = squares + after * after
        norm_next = total(squares)
        share = norm_next / norm_now
        for t, v in fields:
            direction[t, v] = image[t, v] + share * current[t, v]
            right[t, v] = image[t, v]
        norm_now = norm_next
        current = direction


def bits(count):
    return [1 << k for k in range(count.bit_length() - 1)]


def swapped(x, axis, bit):
    return lax.ppermute(x, axis, [(i, i ^ bit) for i in range(lax.axis_size(axis))])


def per_device(class_ids, coef_table, land_mask, cross_cov, time_metric, obs_values, obs_weight, obs_cells, obs_count, block_owner):
    n_lat, n_lon, n_tm = (lax.axis_size(axis) for axis in ("lat", "lon", "tm"))
    rows, cols = class_ids.shape[1:]
    variables = obs_values.shape[1]
    stats = variables + 1
    vmem, smem = pl.BlockSpec(memory_space=pltpu.VMEM), pl.BlockSpec(memory_space=pltpu.SMEM)
    half = jax.ShapeDtypeStruct((n_lon // 2, stats, n_lat, rows, cols), jnp.float32)
    values = obs_values.transpose(1, 0, 2)
    arguments = (block_owner[:, 0], obs_count, coef_table, values, obs_weight, obs_cells, class_ids, land_mask)
    places = [pltpu.SMEM] * 3 + [pltpu.VMEM] * 5
    keep, send, planes = pl.pallas_call(
        tile_kernel,
        out_shape=(half, half, jax.ShapeDtypeStruct((1, n_lat, rows, cols), jnp.float32)),
        in_specs=[pl.BlockSpec(memory_space=pltpu.HBM)] * INPUTS,
        out_specs=(vmem, vmem, vmem),
        scratch_shapes=[
            pltpu.VMEM((n_lon, n_lat, stats, rows, cols), jnp.float32),
            *[place(x.shape, x.dtype) for place, x in zip(places, arguments)],
            pltpu.SemaphoreType.DMA((INPUTS,)),
        ],
        compiler_params=pltpu.CompilerParams(vmem_limit_bytes=32 * 1024 * 1024),
    )(*[pltpu.with_memory_space_constraint(x, pltpu.HBM) for x in arguments])

    partial = keep + swapped(send, "lon", 1)
    for bit in bits(n_lon)[1:]:
        partial = partial[0::2] + swapped(partial[1::2], "lon", bit)
    strip = jnp.concatenate([partial[0], planes], axis=0)
    for bit in bits(n_lat):
        strip = strip + swapped(strip, "lat", bit)

    near, offsets = strip[None], [(0, 0)]
    for bit in bits(n_tm):
        near = jnp.concatenate([near, swapped(near, "tm", bit)], axis=0)
        offsets = offsets + [(j, t + bit) for j, t in offsets]
    for bit in bits(n_lon)[1:]:
        near = jnp.concatenate([near, swapped(near, "lon", bit)], axis=0)
        offsets = offsets + [(j + bit, t) for j, t in offsets]
    far = swapped(near, "lon", 1)

    height, width = n_lat * rows, n_lon * cols
    field = pltpu.VMEM((n_tm, variables, height, width), jnp.float32)
    plane = pltpu.VMEM((n_tm, height, width), jnp.float32)
    out = jax.ShapeDtypeStruct((1, variables, 1, rows, cols), jnp.float32)
    return pl.pallas_call(
        functools.partial(descent_kernel, offsets),
        out_shape=(out, out),
        in_specs=[smem, smem, vmem, vmem],
        out_specs=(vmem, vmem),
        scratch_shapes=[field, field, field, plane, pltpu.VMEM((5, height, width), jnp.float32), plane],
        compiler_params=pltpu.CompilerParams(vmem_limit_bytes=48 * 1024 * 1024),
    )(cross_cov, time_metric, near, far)


def solution(mesh):
    in_specs = (
        P(None, "lat", "lon"),
        P(),
        P(None, "lat", "lon"),
        P(),
        P(),
        P(ALL, None, None),
        P(ALL, None),
        P(ALL, None),
        P(ALL),
        P(ALL, None),
    )
    out_specs = (P("tm", None, None, "lat", "lon"), P("tm", None, None, "lat", "lon"))
    return jax.shard_map(per_device, mesh=mesh, in_specs=in_specs, out_specs=out_specs, check_vma=False)
```

```python
import functools

import jax
import jax.numpy as jnp
from jax import lax
from jax.experimental import pallas as pl
from jax.experimental.pallas import tpu as pltpu
from jax.sharding import PartitionSpec as P

GROUP = 8
SIDES = 4
INPUTS = 8
ALL = ("lat", "lon", "tm")


def exact_dot(x, ones):
    high = x.astype(jnp.bfloat16)
    rest = x - high.astype(jnp.float32)
    middle = rest.astype(jnp.bfloat16)
    low = (rest - middle.astype(jnp.float32)).astype(jnp.bfloat16)
    parts = jnp.dot(jnp.concatenate([high, middle, low], axis=0), ones, preferred_element_type=jnp.float32)
    count = x.shape[0]
    return parts[:count] + (parts[count : 2 * count] + parts[2 * count :])


def side_column(side, cols):
    return jnp.where(side < 2, side, side + cols - SIDES)


def edge_columns(height, cols):
    column = lax.broadcasted_iota(jnp.int32, (cols, SIDES * height), 0)
    side = lax.broadcasted_iota(jnp.int32, (cols, SIDES * height), 1) // height
    return jnp.where(column == side_column(side, cols), 1.0, 0.0).astype(jnp.bfloat16)


def tile_kernel(*refs):
    arguments, (keep_ref, send_ref, planes_ref, tiles) = refs[:INPUTS], refs[INPUTS : INPUTS + 4]
    local, arrived = refs[INPUTS + 4 : -1], refs[-1]
    owner_ref, count_ref, table_ref, values_ref, weight_ref, cells_ref, class_ref, land_ref = local
    copies = [pltpu.make_async_copy(a, b, arrived.at[k]) for k, (a, b) in enumerate(zip(arguments, local))]
    for copy in copies:
        copy.start()
    tiles[...] = jnp.zeros_like(tiles)
    planes_ref[...] = jnp.zeros_like(planes_ref)
    variables, block_total, slots = values_ref.shape
    n_lon, n_lat, stats, rows, cols = tiles.shape
    lat, lon, tm = lax.axis_index("lat"), lax.axis_index("lon"), lax.axis_index("tm")
    for copy in copies:
        copy.wait()

    diffusivity = jnp.zeros((rows, cols), jnp.float32)
    for index in range(table_ref.shape[0]):
        diffusivity = jnp.where(class_ref[0] == index, table_ref[index], diffusivity)
    sea = land_ref[0].astype(jnp.float32)
    plane = jnp.where(tm == 0, diffusivity, sea)
    planes_ref[lat] = plane

    lane = lax.broadcasted_iota(jnp.int32, (1, slots), 1)
    row_ids = lax.broadcasted_iota(jnp.int32, (rows, slots), 0)
    col_ids = lax.broadcasted_iota(jnp.int32, (cols, slots), 0)

    def block_sum(block):
        live = jnp.where(lane < count_ref[block], weight_ref[pl.ds(block, 1), :], 0.0)
        cells = cells_ref[pl.ds(block, 1), :]
        row_hit = row_ids == cells // cols
        terms = [live] + [live * values_ref[v, pl.ds(block, 1), :] for v in range(variables)]
        spread = jnp.concatenate([jnp.where(row_hit, term, 0.0) for term in terms], axis=0)
        high = spread.astype(jnp.bfloat16)
        low = (spread - high.astype(jnp.float32)).astype(jnp.bfloat16)
        col_hot = jnp.where(col_ids == cells % cols, 1.0, 0.0).astype(jnp.bfloat16)
        both = lax.dot_general(
            jnp.concatenate([high, low], axis=0),
            col_hot,
            (((1,), (1,)), ((), ())),
            preferred_element_type=jnp.float32,
        )
        return (both[: stats * rows] + both[stats * rows :]).reshape(stats, rows, cols)

    def step(group, carry):
        sums = [block_sum(group * GROUP + k) for k in range(GROUP)]
        for k in range(GROUP):
            owner = owner_ref[group * GROUP + k]
            tiles[jnp.bitwise_xor(owner % n_lon, lon), owner // n_lon] += sums[k]
        return carry

    lax.fori_loop(0, block_total // GROUP, step, 0)
    for m in range(n_lon // 2):
        for i in range(n_lat):
            for s in range(stats):
                spot = (m * stats + s) * n_lat + i
                keep_ref[spot] = tiles[2 * m, i, s]
                send_ref[spot] = tiles[2 * m + 1, i, s]

    height = n_lat * rows
    lanes = SIDES * height
    edges = edge_columns(height, cols)
    row = lax.broadcasted_iota(jnp.int32, (height, lanes), 0)
    at_row = lax.broadcasted_iota(jnp.int32, (height, lanes), 1) % height == row
    own_row = lax.broadcasted_iota(jnp.int32, (rows, lanes), 1) % height == lax.broadcasted_iota(jnp.int32, (rows, lanes), 0) + lat * rows
    first = n_lon // 2 * stats * n_lat
    chunks = lanes // cols
    for offset in range(n_lon):
        picked = exact_dot(jnp.concatenate([tiles[offset, i, s] for s in range(stats) for i in range(n_lat)], axis=0), edges)
        packed = [
            jnp.sum(jnp.where(at_row, picked[s * height : (s + 1) * height], 0.0), axis=0, keepdims=True) for s in range(stats)
        ]
        blank = jnp.zeros((1, lanes), jnp.float32)
        shared = jnp.sum(jnp.where(own_row, exact_dot(plane, edges), 0.0), axis=0, keepdims=True) if offset == 0 else blank
        packed = jnp.concatenate(packed + [shared] + [blank] * (rows - stats - 1), axis=0)
        for c in range(chunks):
            spot = first + jnp.bitwise_xor(lon, offset) * chunks + c
            keep_ref[spot] = packed[:, c * cols : (c + 1) * cols]
            send_ref[spot] = packed[:, c * cols : (c + 1) * cols]


def strip_kernel(offsets, cov_ref, metric_ref, near_ref, far_ref, own_ref, sums_ref, right, image, change, diag, coef, shared):
    rows, cols = near_ref.shape[2:]
    n_tm, variables, height, width = right.shape
    stats, n_lat, lanes = variables + 1, height // rows, SIDES * height
    lat, lon, tm = lax.axis_index("lat"), lax.axis_index("lon"), lax.axis_index("tm")
    n_lon = lax.axis_size("lon")
    chunks = lanes // cols
    first = (stats + 1) * n_lat
    after, before = lax.rem(lon + 1, n_lon), lax.rem(lon + n_lon - 1, n_lon)
    lane = lax.broadcasted_iota(jnp.int32, (height, lanes), 1)
    at_row = lane % height == lax.broadcasted_iota(jnp.int32, (height, lanes), 0)
    from_after = lax.broadcasted_iota(jnp.int32, (rows, lanes), 1) < 2 * height
    side = lax.broadcasted_iota(jnp.int32, (lanes, cols), 0) // height
    column = lax.broadcasted_iota(jnp.int32, (lanes, cols), 1)
    targets = jnp.where(column == side_column(side, cols), 1.0, 0.0).astype(jnp.bfloat16)

    def place(part_ref, part, tm_offset):
        t = jnp.bitwise_xor(tm, tm_offset)
        for i in range(n_lat):
            down = slice(i * rows, (i + 1) * rows)
            diag[t, down, :cols] = part_ref[part, i]
            for v in range(variables):
                right[t, v, down, :cols] = part_ref[part, (v + 1) * n_lat + i]
            shared[t, down, :cols] = part_ref[part, stats * n_lat + i]

        def packed(j):
            return jnp.concatenate([part_ref[part, first + j * chunks + c] for c in range(chunks)], axis=1)

        beside = jnp.where(from_after, packed(after), packed(before))
        spread = jnp.concatenate([jnp.where(at_row, beside[s : s + 1], 0.0) for s in range(stats + 1)], axis=0)
        columns = exact_dot(spread, targets)
        diag[t, :, cols:] = columns[:height]
        for v in range(variables):
            right[t, v, :, cols:] = columns[(v + 1) * height : (v + 2) * height]
        shared[t, :, cols:] = columns[stats * height :]

    for part, tm_offset in enumerate(offsets):
        place(near_ref, part, tm_offset)
        place(far_ref, part, tm_offset + 1)

    def moved(x, dim, forward):
        return pltpu.roll(x, 1 if forward else x.shape[dim] - 1, dim)

    diffusivity, sea = shared[0], shared[1]
    row_ids = lax.broadcasted_iota(jnp.int32, (height, width), 0)
    north_open, south_open = row_ids > 0, row_ids < height - 1
    north = 0.5 * (jnp.where(north_open, moved(diffusivity, 0, True), 0.0) + diffusivity)
    south = 0.5 * (diffusivity + jnp.where(south_open, moved(diffusivity, 0, False), 0.0))
    west = 0.5 * (moved(diffusivity, 1, True) + diffusivity)
    east = 0.5 * (diffusivity + moved(diffusivity, 1, False))
    coef[0] = jnp.where(north_open, north, 0.0)
    coef[1] = jnp.where(south_open, south, 0.0)
    coef[2] = west
    coef[3] = east
    coef[4] = north + south + west + east

    def operate(field, span, use):
        sea = shared[1]
        for t in range(n_tm):
            masked = [[field[s, v] * sea for v in range(variables)] for s in range(n_tm)]
            centre = (diag[t] + coef[4])[:, :span]
            for v in range(variables):
                here = masked[t][v]
                mixed = centre * here[:, :span]
                for w in range(variables):
                    mixed = mixed + cov_ref[v, w] * masked[t][w][:, :span]
                for s in range(n_tm):
                    mixed = mixed + metric_ref[t, s] * masked[s][v][:, :span]
                spread = (
                    coef[0, :, :span] * moved(here[:, :span], 0, True)
                    + coef[1, :, :span] * moved(here[:, :span], 0, False)
                    + coef[2, :, :span] * moved(here, 1, True)[:, :span]
                    + coef[3, :, :span] * moved(here, 1, False)[:, :span]
                )
                use(t, v, sea[:, :span] * (mixed - spread) + (1.0 - sea[:, :span]) * field[t, v, :, :span])

    def sum_of(products):
        return jnp.sum(jnp.sum(products, axis=1, keepdims=True), axis=0, keepdims=True)

    fields = [(t, v) for t in range(n_tm) for v in range(variables)]
    none = jnp.zeros((height, cols), jnp.float32)
    bb, bw, ww, uu, ub, us, cross = [none] * 7
    for t, v in fields:
        start = sea * right[t, v]
        right[t, v] = start
        bb = bb + start[:, :cols] * start[:, :cols]

    def first_image(t, v, result):
        nonlocal bw, ww
        image[t, v] = result
        here = result[:, :cols]
        bw = bw + right[t, v, :, :cols] * here
        ww = ww + here * here

    operate(right, width, first_image)
    bb, ww = sum_of(bb), sum_of(ww)
    usable = (bb > 0.0) & (ww > 0.0)
    alpha = jnp.where(usable, jnp.sqrt(bb / jnp.where(usable, ww, 1.0)), 1.0)
    for t, v in fields:
        start = right[t, v]
        left = start - alpha * image[t, v]
        change[t, v] = left
        left, start = left[:, :cols], start[:, :cols]
        uu = uu + left * left
        ub = ub + left * start

    def second_image(t, v, result):
        nonlocal us, cross
        left, start = change[t, v, :, :cols], right[t, v, :, :cols]
        us = us + left * result
        cross = cross + (left * image[t, v, :, :cols] + start * result)
        image[t, v, :, cols:] = result

    operate(change, cols, second_image)
    own_rows = pl.ds(pl.multiple_of(lat * rows, rows), rows)
    for v in range(variables):
        own_ref[0, v] = right[tm, v, own_rows, :cols]
        own_ref[1, v] = image[tm, v, own_rows, :cols]
        own_ref[2, v] = change[tm, v, own_rows, :cols]
        own_ref[3, v] = image[tm, v, own_rows, cols:]
    for k, value in enumerate((alpha, bb, sum_of(bw), sum_of(uu), sum_of(ub), sum_of(us), sum_of(cross))):
        sums_ref[0, k : k + 1] = jnp.broadcast_to(value, (1, cols))
    sums_ref[0, 7:8] = jnp.zeros((1, cols), jnp.float32)


def update_kernel(own_ref, mine_ref, near_ref, far_ref, solution_ref, residual_ref):
    devices = [near_ref[k] for k in range(near_ref.shape[0])] + [far_ref[k] for k in range(far_ref.shape[0])]

    def over(values):
        return functools.reduce(jnp.add, values)

    def sums(device):
        return [device[k : k + 1] for k in range(7)]

    norm_start = over([sums(d)[1] for d in devices])
    step_first = norm_start / over([sums(d)[2] for d in devices])
    squares = []
    for d in devices:
        alpha, bb, bw, uu, ub, us, cross = sums(d)
        rho = step_first / alpha
        squares.append(rho * rho * uu + 2.0 * rho * (1.0 - rho) * ub + (1.0 - rho) * (1.0 - rho) * bb)
    norm_next = over(squares)
    share = norm_next / norm_start
    products = []
    for d in devices:
        alpha, bb, bw, uu, ub, us, cross = sums(d)
        rho = step_first / alpha
        kappa = 1.0 - rho + share
        products.append(rho * rho * us + rho * kappa * cross + kappa * kappa * bw)
    step_second = norm_next / over(products)
    rho = step_first / mine_ref[0, 0:1]
    kappa = 1.0 - rho + share
    for v in range(own_ref.shape[1]):
        start, image, left, left_image = (own_ref[k, v] for k in range(4))
        solution_ref[0, v, 0] = step_first * start + step_second * (rho * left + kappa * start)
        residual_ref[0, v, 0] = rho * left + (1.0 - rho) * start - step_second * (rho * left_image + kappa * image)


def bits(count):
    return [1 << k for k in range(count.bit_length() - 1)]


def swapped(x, axis, bit):
    return lax.ppermute(x, axis, [(i, i ^ bit) for i in range(lax.axis_size(axis))])


def gathered(x, axis):
    near, offsets = x[None], [0]
    for bit in reversed(bits(lax.axis_size(axis))[1:]):
        near = jnp.concatenate([near, swapped(near, axis, bit)], axis=0)
        offsets = offsets + [j + bit for j in offsets]
    return near, swapped(near, axis, 1), offsets


def per_device(class_ids, coef_table, land_mask, cross_cov, time_metric, obs_values, obs_weight, obs_cells, obs_count, block_owner):
    n_lat, n_lon, n_tm = (lax.axis_size(axis) for axis in ("lat", "lon", "tm"))
    rows, cols = class_ids.shape[1:]
    variables = obs_values.shape[1]
    stats = variables + 1
    vmem, smem = pl.BlockSpec(memory_space=pltpu.VMEM), pl.BlockSpec(memory_space=pltpu.SMEM)
    height = n_lat * rows
    halo = n_lon * SIDES * height // cols
    half = jax.ShapeDtypeStruct((n_lon // 2 * stats * n_lat + halo, rows, cols), jnp.float32)
    values = obs_values.transpose(1, 0, 2)
    arguments = (block_owner[:, 0], obs_count, coef_table, values, obs_weight, obs_cells, class_ids, land_mask)
    places = [pltpu.SMEM] * 3 + [pltpu.VMEM] * 5
    keep, send, planes = pl.pallas_call(
        tile_kernel,
        out_shape=(half, half, jax.ShapeDtypeStruct((n_lat, rows, cols), jnp.float32)),
        in_specs=[pl.BlockSpec(memory_space=pltpu.HBM)] * INPUTS,
        out_specs=(vmem, vmem, vmem),
        scratch_shapes=[
            pltpu.VMEM((n_lon, n_lat, stats, rows, cols), jnp.float32),
            *[place(x.shape, x.dtype) for place, x in zip(places, arguments)],
            pltpu.SemaphoreType.DMA((INPUTS,)),
        ],
        compiler_params=pltpu.CompilerParams(vmem_limit_bytes=32 * 1024 * 1024),
    )(*[pltpu.with_memory_space_constraint(x, pltpu.HBM) for x in arguments])

    partial = keep + swapped(send, "lon", 1)
    body, sides = partial[:-halo].reshape(n_lon // 2, stats * n_lat, rows, cols), partial[-halo:]
    for bit in bits(n_lon)[1:]:
        count = body.shape[0] // 2
        given = swapped(jnp.concatenate([body[1::2].reshape(-1, rows, cols), sides], axis=0), "lon", bit)
        body = body[0::2] + given[:-halo].reshape(count, stats * n_lat, rows, cols)
        sides = sides + given[-halo:]
    strip = jnp.concatenate([body[0], planes, sides], axis=0)
    for bit in bits(n_lat):
        strip = strip + swapped(strip, "lat", bit)

    near, far, offsets = gathered(strip, "tm")
    field = pltpu.VMEM((n_tm, variables, height, 2 * cols), jnp.float32)
    plane = pltpu.VMEM((n_tm, height, 2 * cols), jnp.float32)
    own, sums = pl.pallas_call(
        functools.partial(strip_kernel, offsets),
        out_shape=(
            jax.ShapeDtypeStruct((4, variables, rows, cols), jnp.float32),
            jax.ShapeDtypeStruct((1, rows, cols), jnp.float32),
        ),
        in_specs=[smem, smem, vmem, vmem],
        out_specs=(vmem, vmem),
        scratch_shapes=[field, field, field, plane, pltpu.VMEM((5, height, 2 * cols), jnp.float32), plane],
        compiler_params=pltpu.CompilerParams(vmem_limit_bytes=24 * 1024 * 1024),
    )(cross_cov, time_metric, near, far)

    near, far, _ = gathered(sums[0], "lon")
    out = jax.ShapeDtypeStruct((1, variables, 1, rows, cols), jnp.float32)
    return pl.pallas_call(
        update_kernel,
        out_shape=(out, out),
        in_specs=[vmem] * 4,
        out_specs=(vmem, vmem),
        compiler_params=pltpu.CompilerParams(vmem_limit_bytes=8 * 1024 * 1024),
    )(own, sums, near, far)


def solution(mesh):
    in_specs = (
        P(None, "lat", "lon"),
        P(),
        P(None, "lat", "lon"),
        P(),
        P(),
        P(ALL, None, None),
        P(ALL, None),
        P(ALL, None),
        P(ALL),
        P(ALL, None),
    )
    out_specs = (P("tm", None, None, "lat", "lon"), P("tm", None, None, "lat", "lon"))
    return jax.shard_map(per_device, mesh=mesh, in_specs=in_specs, out_specs=out_specs, check_vma=False)
```

```python
import functools

import jax
import jax.numpy as jnp
from jax import lax
from jax.experimental import pallas as pl
from jax.experimental.pallas import tpu as pltpu
from jax.sharding import PartitionSpec as P

GROUP = 64
SIDES = 4
INPUTS = 8
ALL = ("lat", "lon", "tm")


def exact_dot(x, ones):
    high = x.astype(jnp.bfloat16)
    rest = x - high.astype(jnp.float32)
    middle = rest.astype(jnp.bfloat16)
    low = (rest - middle.astype(jnp.float32)).astype(jnp.bfloat16)
    parts = jnp.dot(jnp.concatenate([high, middle, low], axis=0), ones, preferred_element_type=jnp.float32)
    count = x.shape[0]
    return parts[:count] + (parts[count : 2 * count] + parts[2 * count :])


def side_column(side, cols):
    return jnp.where(side < 2, side, side + cols - SIDES)


def edge_columns(height, cols):
    column = lax.broadcasted_iota(jnp.int32, (cols, SIDES * height), 0)
    side = lax.broadcasted_iota(jnp.int32, (cols, SIDES * height), 1) // height
    return jnp.where(column == side_column(side, cols), 1.0, 0.0).astype(jnp.bfloat16)


def tile_kernel(*refs):
    arguments, (keep_ref, send_ref, planes_ref, tiles, packed) = refs[:INPUTS], refs[INPUTS : INPUTS + 5]
    local, arrived = refs[INPUTS + 5 : -1], refs[-1]
    owner_ref, count_ref, table_ref, values_ref, weight_ref, cells_ref, class_ref, land_ref = local
    copies = [pltpu.make_async_copy(a, b, arrived.at[k]) for k, (a, b) in enumerate(zip(arguments, local))]
    for copy in copies:
        copy.start()
    tiles[...] = jnp.zeros_like(tiles)
    planes_ref[...] = jnp.zeros_like(planes_ref)
    variables, block_total, slots = values_ref.shape
    n_lon, n_lat, stats, rows, cols = tiles.shape
    lat, lon, tm = lax.axis_index("lat"), lax.axis_index("lon"), lax.axis_index("tm")
    for copy in copies:
        copy.wait()

    diffusivity = jnp.zeros((rows, cols), jnp.float32)
    for index in range(table_ref.shape[0]):
        diffusivity = jnp.where(class_ref[0] == index, table_ref[index], diffusivity)
    sea = land_ref[0].astype(jnp.float32)
    plane = jnp.where(tm == 0, diffusivity, sea)
    planes_ref[lat] = plane

    lane = lax.broadcasted_iota(jnp.int32, (1, slots), 1)
    row_ids = lax.broadcasted_iota(jnp.int32, (rows, slots), 0)
    col_ids = lax.broadcasted_iota(jnp.int32, (cols, slots), 0)

    nothing = jnp.zeros((2 * stats * rows, slots), jnp.bfloat16)

    def operands(block):
        live = jnp.where(lane < count_ref[block], weight_ref[pl.ds(block, 1), :], 0.0)
        cells = cells_ref[pl.ds(block, 1), :]
        row_hit = row_ids == cells // cols
        terms = [live] + [live * values_ref[v, pl.ds(block, 1), :] for v in range(variables)]
        high = [term.astype(jnp.bfloat16).astype(jnp.float32) for term in terms]
        low = [term - part for term, part in zip(terms, high)]
        spread = jnp.concatenate([jnp.where(row_hit, part, 0.0) for part in high + low], axis=0)
        return spread.astype(jnp.bfloat16), jnp.where(col_ids == cells % cols, 1.0, 0.0).astype(jnp.bfloat16)

    def pair_sums(block):
        (first, first_hot), (second, second_hot) = operands(block), operands(block + 1)
        both = lax.dot_general(
            jnp.concatenate([jnp.concatenate([first, nothing], axis=1), jnp.concatenate([nothing, second], axis=1)], axis=0),
            jnp.concatenate([first_hot, second_hot], axis=1),
            (((1,), (1,)), ((), ())),
            preferred_element_type=jnp.float32,
        ).reshape(2, 2, stats, rows, cols)
        return [both[0, 0] + both[0, 1], both[1, 0] + both[1, 1]]

    def step(group, carry):
        sums = []
        for k in range(0, GROUP, 2):
            sums += pair_sums(group * GROUP + k)
        for k in range(GROUP):
            owner = owner_ref[group * GROUP + k]
            tiles[jnp.bitwise_xor(owner % n_lon, lon), owner // n_lon] += sums[k]
        return carry

    lax.fori_loop(0, block_total // GROUP, step, 0)
    own_tiles = stats * n_lat
    for m in range(n_lon // 2):
        for i in range(n_lat):
            for s in range(stats):
                keep_ref[m, s * n_lat + i] = tiles[2 * m, i, s]
                send_ref[m, s * n_lat + i] = tiles[2 * m + 1, i, s]

    height = n_lat * rows
    lanes = SIDES * height
    edges = edge_columns(height, cols)
    row = lax.broadcasted_iota(jnp.int32, (height, lanes), 0)
    at_row = lax.broadcasted_iota(jnp.int32, (height, lanes), 1) % height == row
    own_row = lax.broadcasted_iota(jnp.int32, (rows, lanes), 1) % height == lax.broadcasted_iota(jnp.int32, (rows, lanes), 0) + lat * rows
    blank = jnp.zeros((1, lanes), jnp.float32)
    for offset in range(n_lon):
        picked = exact_dot(jnp.concatenate([tiles[offset, i, s] for s in range(stats) for i in range(n_lat)], axis=0), edges)
        rows_of = [jnp.where(at_row, picked[s * height : (s + 1) * height], 0.0) for s in range(stats)]
        rows_of.append(jnp.where(own_row, exact_dot(plane, edges), 0.0) if offset == 0 else blank)
        sums = [jnp.sum(x, axis=0, keepdims=True) for x in rows_of]
        packed[offset] = jnp.concatenate(sums + [blank] * (rows - stats - 1), axis=0)
    from_after = lax.broadcasted_iota(jnp.int32, (rows, lanes), 1) < 2 * height
    for offset in range(n_lon):
        target = jnp.bitwise_xor(lon, offset)
        after = jnp.bitwise_xor(lon, lax.rem(target + 1, n_lon))
        before = jnp.bitwise_xor(lon, lax.rem(target + n_lon - 1, n_lon))
        beside = jnp.where(from_after, packed[after], packed[before])
        out_ref = send_ref if offset % 2 else keep_ref
        for c in range(lanes // cols):
            out_ref[offset // 2, own_tiles + c] = beside[:, c * cols : (c + 1) * cols]


def strip_kernel(offsets, cov_ref, metric_ref, near_ref, far_ref, own_ref, sums_ref, right, image, change, diag, coef, shared):
    rows, cols = near_ref.shape[2:]
    n_tm, variables, height, width = right.shape
    stats, n_lat, lanes = variables + 1, height // rows, SIDES * height
    lat, tm = lax.axis_index("lat"), lax.axis_index("tm")
    chunks = lanes // cols
    first = stats * n_lat
    lane = lax.broadcasted_iota(jnp.int32, (height, lanes), 1)
    at_row = lane % height == lax.broadcasted_iota(jnp.int32, (height, lanes), 0)
    side = lax.broadcasted_iota(jnp.int32, (lanes, cols), 0) // height
    column = lax.broadcasted_iota(jnp.int32, (lanes, cols), 1)
    targets = jnp.where(column == side_column(side, cols), 1.0, 0.0).astype(jnp.bfloat16)

    def place(part_ref, part, tm_offset):
        t = jnp.bitwise_xor(tm, tm_offset)
        for i in range(n_lat):
            down = slice(i * rows, (i + 1) * rows)
            diag[t, down, :cols] = part_ref[part, i]
            for v in range(variables):
                right[t, v, down, :cols] = part_ref[part, (v + 1) * n_lat + i]
            shared[t, down, :cols] = part_ref[part, first + chunks + i]

        beside = jnp.concatenate([part_ref[part, first + c] for c in range(chunks)], axis=1)
        spread = jnp.concatenate([jnp.where(at_row, beside[s : s + 1], 0.0) for s in range(stats + 1)], axis=0)
        columns = exact_dot(spread, targets)
        diag[t, :, cols:] = columns[:height]
        for v in range(variables):
            right[t, v, :, cols:] = columns[(v + 1) * height : (v + 2) * height]
        shared[t, :, cols:] = columns[stats * height :]

    for part, tm_offset in enumerate(offsets):
        place(near_ref, part, tm_offset)
        place(far_ref, part, tm_offset + 1)

    def moved(x, dim, forward):
        return pltpu.roll(x, 1 if forward else x.shape[dim] - 1, dim)

    diffusivity, sea = shared[0], shared[1]
    row_ids = lax.broadcasted_iota(jnp.int32, (height, width), 0)
    north_open, south_open = row_ids > 0, row_ids < height - 1
    north = 0.5 * (jnp.where(north_open, moved(diffusivity, 0, True), 0.0) + diffusivity)
    south = 0.5 * (diffusivity + jnp.where(south_open, moved(diffusivity, 0, False), 0.0))
    west = 0.5 * (moved(diffusivity, 1, True) + diffusivity)
    east = 0.5 * (diffusivity + moved(diffusivity, 1, False))
    coef[0] = jnp.where(north_open, north, 0.0)
    coef[1] = jnp.where(south_open, south, 0.0)
    coef[2] = west
    coef[3] = east
    coef[4] = north + south + west + east

    def operate(field, span, use):
        sea = shared[1]
        for t in range(n_tm):
            masked = [[field[s, v] * sea for v in range(variables)] for s in range(n_tm)]
            centre = (diag[t] + coef[4])[:, :span]
            for v in range(variables):
                here = masked[t][v]
                mixed = centre * here[:, :span]
                for w in range(variables):
                    mixed = mixed + cov_ref[v, w] * masked[t][w][:, :span]
                for s in range(n_tm):
                    mixed = mixed + metric_ref[t, s] * masked[s][v][:, :span]
                spread = (
                    coef[0, :, :span] * moved(here[:, :span], 0, True)
                    + coef[1, :, :span] * moved(here[:, :span], 0, False)
                    + coef[2, :, :span] * moved(here, 1, True)[:, :span]
                    + coef[3, :, :span] * moved(here, 1, False)[:, :span]
                )
                use(t, v, sea[:, :span] * (mixed - spread) + (1.0 - sea[:, :span]) * field[t, v, :, :span])

    def sum_of(products):
        return jnp.sum(jnp.sum(products, axis=1, keepdims=True), axis=0, keepdims=True)

    fields = [(t, v) for t in range(n_tm) for v in range(variables)]
    none = jnp.zeros((height, cols), jnp.float32)
    bb, bw, ww, uu, ub, us, cross = [none] * 7
    for t, v in fields:
        start = sea * right[t, v]
        right[t, v] = start
        bb = bb + start[:, :cols] * start[:, :cols]

    def first_image(t, v, result):
        nonlocal bw, ww
        image[t, v] = result
        here = result[:, :cols]
        bw = bw + right[t, v, :, :cols] * here
        ww = ww + here * here

    operate(right, width, first_image)
    bb, ww = sum_of(bb), sum_of(ww)
    usable = (bb > 0.0) & (ww > 0.0)
    alpha = jnp.where(usable, jnp.sqrt(bb / jnp.where(usable, ww, 1.0)), 1.0)
    for t, v in fields:
        start = right[t, v]
        left = start - alpha * image[t, v]
        change[t, v] = left
        left, start = left[:, :cols], start[:, :cols]
        uu = uu + left * left
        ub = ub + left * start

    def second_image(t, v, result):
        nonlocal us, cross
        left, start = change[t, v, :, :cols], right[t, v, :, :cols]
        us = us + left * result
        cross = cross + (left * image[t, v, :, :cols] + start * result)
        image[t, v, :, cols:] = result

    operate(change, cols, second_image)
    own_rows = pl.ds(pl.multiple_of(lat * rows, rows), rows)
    for v in range(variables):
        own_ref[0, v] = right[tm, v, own_rows, :cols]
        own_ref[1, v] = image[tm, v, own_rows, :cols]
        own_ref[2, v] = change[tm, v, own_rows, :cols]
        own_ref[3, v] = image[tm, v, own_rows, cols:]
    for k, value in enumerate((alpha, bb, sum_of(bw), sum_of(uu), sum_of(ub), sum_of(us), sum_of(cross))):
        sums_ref[0, k : k + 1] = jnp.broadcast_to(value, (1, cols))
    sums_ref[0, 7:8] = jnp.zeros((1, cols), jnp.float32)


def update_kernel(own_ref, mine_ref, near_ref, far_ref, solution_ref, residual_ref):
    devices = [near_ref[k] for k in range(near_ref.shape[0])] + [far_ref[k] for k in range(far_ref.shape[0])]

    def over(values):
        return functools.reduce(jnp.add, values)

    def sums(device):
        return [device[k : k + 1] for k in range(7)]

    norm_start = over([sums(d)[1] for d in devices])
    step_first = norm_start / over([sums(d)[2] for d in devices])
    squares = []
    for d in devices:
        alpha, bb, bw, uu, ub, us, cross = sums(d)
        rho = step_first / alpha
        squares.append(rho * rho * uu + 2.0 * rho * (1.0 - rho) * ub + (1.0 - rho) * (1.0 - rho) * bb)
    norm_next = over(squares)
    share = norm_next / norm_start
    products = []
    for d in devices:
        alpha, bb, bw, uu, ub, us, cross = sums(d)
        rho = step_first / alpha
        kappa = 1.0 - rho + share
        products.append(rho * rho * us + rho * kappa * cross + kappa * kappa * bw)
    step_second = norm_next / over(products)
    rho = step_first / mine_ref[0, 0:1]
    kappa = 1.0 - rho + share
    for v in range(own_ref.shape[1]):
        start, image, left, left_image = (own_ref[k, v] for k in range(4))
        solution_ref[0, v, 0] = step_first * start + step_second * (rho * left + kappa * start)
        residual_ref[0, v, 0] = rho * left + (1.0 - rho) * start - step_second * (rho * left_image + kappa * image)


def bits(count):
    return [1 << k for k in range(count.bit_length() - 1)]


def swapped(x, axis, bit):
    return lax.ppermute(x, axis, [(i, i ^ bit) for i in range(lax.axis_size(axis))])


def gathered(x, axis):
    near, offsets = x[None], [0]
    for bit in reversed(bits(lax.axis_size(axis))[1:]):
        near = jnp.concatenate([near, swapped(near, axis, bit)], axis=0)
        offsets = offsets + [j + bit for j in offsets]
    return near, swapped(near, axis, 1), offsets


def per_device(class_ids, coef_table, land_mask, cross_cov, time_metric, obs_values, obs_weight, obs_cells, obs_count, block_owner):
    n_lat, n_lon, n_tm = (lax.axis_size(axis) for axis in ("lat", "lon", "tm"))
    rows, cols = class_ids.shape[1:]
    variables = obs_values.shape[1]
    stats = variables + 1
    vmem, smem = pl.BlockSpec(memory_space=pltpu.VMEM), pl.BlockSpec(memory_space=pltpu.SMEM)
    height = n_lat * rows
    half = jax.ShapeDtypeStruct((n_lon // 2, stats * n_lat + SIDES * height // cols, rows, cols), jnp.float32)
    values = obs_values.transpose(1, 0, 2)
    arguments = (block_owner[:, 0], obs_count, coef_table, values, obs_weight, obs_cells, class_ids, land_mask)
    places = [pltpu.SMEM] * 3 + [pltpu.VMEM] * 5
    keep, send, planes = pl.pallas_call(
        tile_kernel,
        out_shape=(half, half, jax.ShapeDtypeStruct((n_lat, rows, cols), jnp.float32)),
        in_specs=[pl.BlockSpec(memory_space=pltpu.HBM)] * INPUTS,
        out_specs=(vmem, vmem, vmem),
        scratch_shapes=[
            pltpu.VMEM((n_lon, n_lat, stats, rows, cols), jnp.float32),
            pltpu.VMEM((n_lon, rows, SIDES * height), jnp.float32),
            *[place(x.shape, x.dtype) for place, x in zip(places, arguments)],
            pltpu.SemaphoreType.DMA((INPUTS,)),
        ],
        compiler_params=pltpu.CompilerParams(vmem_limit_bytes=32 * 1024 * 1024),
    )(*[pltpu.with_memory_space_constraint(x, pltpu.HBM) for x in arguments])

    partial = keep + swapped(send, "lon", 1)
    for bit in bits(n_lon)[1:]:
        partial = partial[0::2] + swapped(partial[1::2], "lon", bit)
    strip = jnp.concatenate([partial[0], planes], axis=0)
    for bit in bits(n_lat):
        strip = strip + swapped(strip, "lat", bit)

    near, far, offsets = gathered(strip, "tm")
    field = pltpu.VMEM((n_tm, variables, height, 2 * cols), jnp.float32)
    plane = pltpu.VMEM((n_tm, height, 2 * cols), jnp.float32)
    own, sums = pl.pallas_call(
        functools.partial(strip_kernel, offsets),
        out_shape=(
            jax.ShapeDtypeStruct((4, variables, rows, cols), jnp.float32),
            jax.ShapeDtypeStruct((1, rows, cols), jnp.float32),
        ),
        in_specs=[smem, smem, vmem, vmem],
        out_specs=(vmem, vmem),
        scratch_shapes=[field, field, field, plane, pltpu.VMEM((5, height, 2 * cols), jnp.float32), plane],
        compiler_params=pltpu.CompilerParams(vmem_limit_bytes=24 * 1024 * 1024),
    )(cross_cov, time_metric, near, far)

    near, far, _ = gathered(sums[0], "lon")
    out = jax.ShapeDtypeStruct((1, variables, 1, rows, cols), jnp.float32)
    return pl.pallas_call(
        update_kernel,
        out_shape=(out, out),
        in_specs=[vmem] * 4,
        out_specs=(vmem, vmem),
        compiler_params=pltpu.CompilerParams(vmem_limit_bytes=8 * 1024 * 1024),
    )(own, sums, near, far)


def solution(mesh):
    in_specs = (
        P(None, "lat", "lon"),
        P(),
        P(None, "lat", "lon"),
        P(),
        P(),
        P(ALL, None, None),
        P(ALL, None),
        P(ALL, None),
        P(ALL),
        P(ALL, None),
    )
    out_specs = (P("tm", None, None, "lat", "lon"), P("tm", None, None, "lat", "lon"))
    return jax.shard_map(per_device, mesh=mesh, in_specs=in_specs, out_specs=out_specs, check_vma=False)
```

```python
import functools

import jax
import jax.numpy as jnp
from jax import lax
from jax.experimental import pallas as pl
from jax.experimental.pallas import tpu as pltpu
from jax.sharding import PartitionSpec as P

GROUP = 64
SIDES = 4
INPUTS = 10
ALL = ("lat", "lon", "tm")


def exact_dot(x, ones):
    high = x.astype(jnp.bfloat16)
    rest = x - high.astype(jnp.float32)
    middle = rest.astype(jnp.bfloat16)
    low = (rest - middle.astype(jnp.float32)).astype(jnp.bfloat16)
    parts = jnp.dot(jnp.concatenate([high, middle, low], axis=0), ones, preferred_element_type=jnp.float32)
    count = x.shape[0]
    return parts[:count] + (parts[count : 2 * count] + parts[2 * count :])


def side_column(side, cols):
    return jnp.where(side < 2, side, side + cols - SIDES)


def edge_columns(height, cols):
    column = lax.broadcasted_iota(jnp.int32, (cols, SIDES * height), 0)
    side = lax.broadcasted_iota(jnp.int32, (cols, SIDES * height), 1) // height
    return jnp.where(column == side_column(side, cols), 1.0, 0.0).astype(jnp.bfloat16)


def tile_kernel(*refs):
    arguments, (keep_ref, send_ref, plane_ref, factors_ref, tiles, packed) = refs[:INPUTS], refs[INPUTS : INPUTS + 6]
    local, arrived = refs[INPUTS + 6 : -1], refs[-1]
    owner_ref, count_ref, table_ref, cov_ref, metric_ref, values_ref, weight_ref, cells_ref, class_ref, land_ref = local
    copies = [pltpu.make_async_copy(a, b, arrived.at[k]) for k, (a, b) in enumerate(zip(arguments, local))]
    for copy in copies:
        copy.start()
    tiles[...] = jnp.zeros_like(tiles)
    variables, block_total, slots = values_ref.shape
    n_lon, n_lat, stats, rows, cols = tiles.shape
    lat, lon, tm = lax.axis_index("lat"), lax.axis_index("lon"), lax.axis_index("tm")
    for copy in copies:
        copy.wait()

    diffusivity = jnp.zeros((rows, cols), jnp.float32)
    for index in range(table_ref.shape[0]):
        diffusivity = jnp.where(class_ref[0] == index, table_ref[index], diffusivity)
    sea = land_ref[0].astype(jnp.float32)
    plane = jnp.where(tm == 0, diffusivity, sea)
    plane_ref[0] = plane
    months = metric_ref.shape[0]
    for v in range(variables):
        for w in range(variables):
            factors_ref[v * variables + w] = jnp.full(factors_ref.shape[1:], cov_ref[v, w])
    for t in range(months):
        for u in range(months):
            factors_ref[variables * variables + t * months + u] = jnp.full(factors_ref.shape[1:], metric_ref[t, u])

    lane = lax.broadcasted_iota(jnp.int32, (1, slots), 1)
    row_ids = lax.broadcasted_iota(jnp.int32, (rows, slots), 0)
    col_ids = lax.broadcasted_iota(jnp.int32, (cols, slots), 0)

    nothing = jnp.zeros((2 * stats * rows, slots), jnp.bfloat16)

    def operands(block):
        live = jnp.where(lane < count_ref[block], weight_ref[pl.ds(block, 1), :], 0.0)
        cells = cells_ref[pl.ds(block, 1), :]
        row_hit = row_ids == cells // cols
        terms = [live] + [live * values_ref[v, pl.ds(block, 1), :] for v in range(variables)]
        high = [term.astype(jnp.bfloat16).astype(jnp.float32) for term in terms]
        low = [term - part for term, part in zip(terms, high)]
        spread = jnp.concatenate([jnp.where(row_hit, part, 0.0) for part in high + low], axis=0)
        return spread.astype(jnp.bfloat16), jnp.where(col_ids == cells % cols, 1.0, 0.0).astype(jnp.bfloat16)

    def pair_sums(block):
        (first, first_hot), (second, second_hot) = operands(block), operands(block + 1)
        both = lax.dot_general(
            jnp.concatenate([jnp.concatenate([first, nothing], axis=1), jnp.concatenate([nothing, second], axis=1)], axis=0),
            jnp.concatenate([first_hot, second_hot], axis=1),
            (((1,), (1,)), ((), ())),
            preferred_element_type=jnp.float32,
        ).reshape(2, 2, stats, rows, cols)
        return [both[0, 0] + both[0, 1], both[1, 0] + both[1, 1]]

    def step(group, carry):
        sums = []
        for k in range(0, GROUP, 2):
            sums += pair_sums(group * GROUP + k)
        for k in range(GROUP):
            owner = owner_ref[group * GROUP + k]
            tiles[jnp.bitwise_xor(owner % n_lon, lon), owner // n_lon] += sums[k]
        return carry

    lax.fori_loop(0, block_total // GROUP, step, 0)
    own_tiles = stats * n_lat
    for m in range(n_lon // 2):
        for i in range(n_lat):
            for s in range(stats):
                keep_ref[m, s * n_lat + i] = tiles[2 * m, i, s]
                send_ref[m, s * n_lat + i] = tiles[2 * m + 1, i, s]

    height = n_lat * rows
    lanes = SIDES * height
    edges = edge_columns(height, cols)
    row = lax.broadcasted_iota(jnp.int32, (height, lanes), 0)
    at_row = lax.broadcasted_iota(jnp.int32, (height, lanes), 1) % height == row
    own_row = lax.broadcasted_iota(jnp.int32, (rows, lanes), 1) % height == lax.broadcasted_iota(jnp.int32, (rows, lanes), 0) + lat * rows
    blank = jnp.zeros((1, lanes), jnp.float32)
    for offset in range(n_lon):
        picked = exact_dot(jnp.concatenate([tiles[offset, i, s] for s in range(stats) for i in range(n_lat)], axis=0), edges)
        rows_of = [jnp.where(at_row, picked[s * height : (s + 1) * height], 0.0) for s in range(stats)]
        rows_of.append(jnp.where(own_row, exact_dot(plane, edges), 0.0) if offset == 0 else blank)
        sums = [jnp.sum(x, axis=0, keepdims=True) for x in rows_of]
        packed[offset] = jnp.concatenate(sums + [blank] * (rows - stats - 1), axis=0)
    from_after = lax.broadcasted_iota(jnp.int32, (rows, lanes), 1) < 2 * height
    for offset in range(n_lon):
        target = jnp.bitwise_xor(lon, offset)
        after = jnp.bitwise_xor(lon, lax.rem(target + 1, n_lon))
        before = jnp.bitwise_xor(lon, lax.rem(target + n_lon - 1, n_lon))
        beside = jnp.where(from_after, packed[after], packed[before])
        out_ref = send_ref if offset % 2 else keep_ref
        for c in range(lanes // cols):
            out_ref[offset // 2, own_tiles + c] = beside[:, c * cols : (c + 1) * cols]


def strip_kernel(offsets, lat_offsets, factors_ref, near_ref, far_ref, own_ref, sums_ref, right, image, change, diag, coef, shared):
    rows, cols = near_ref.shape[2:]
    n_tm, variables, height, width = right.shape
    stats, n_lat, lanes = variables + 1, height // rows, SIDES * height
    lat, tm = lax.axis_index("lat"), lax.axis_index("tm")
    chunks = lanes // cols
    first = stats * n_lat
    lane = lax.broadcasted_iota(jnp.int32, (height, lanes), 1)
    at_row = lane % height == lax.broadcasted_iota(jnp.int32, (height, lanes), 0)
    side = lax.broadcasted_iota(jnp.int32, (lanes, cols), 0) // height
    column = lax.broadcasted_iota(jnp.int32, (lanes, cols), 1)
    targets = jnp.where(column == side_column(side, cols), 1.0, 0.0).astype(jnp.bfloat16)

    def place(part_ref, part, tm_offset):
        t = jnp.bitwise_xor(tm, tm_offset)
        for i in range(n_lat):
            down = slice(i * rows, (i + 1) * rows)
            diag[t, down, :cols] = part_ref[part, i]
            for v in range(variables):
                right[t, v, down, :cols] = part_ref[part, (v + 1) * n_lat + i]

        for k, offset in enumerate(lat_offsets):
            down = pl.ds(pl.multiple_of(jnp.bitwise_xor(lat, offset) * rows, rows), rows)
            shared[t, down, :cols] = part_ref[part, first + chunks + k]

        beside = jnp.concatenate([part_ref[part, first + c] for c in range(chunks)], axis=1)
        spread = jnp.concatenate([jnp.where(at_row, beside[s : s + 1], 0.0) for s in range(stats + 1)], axis=0)
        columns = exact_dot(spread, targets)
        diag[t, :, cols:] = columns[:height]
        for v in range(variables):
            right[t, v, :, cols:] = columns[(v + 1) * height : (v + 2) * height]
        shared[t, :, cols:] = columns[stats * height :]

    for part, tm_offset in enumerate(offsets):
        place(near_ref, part, tm_offset)
        place(far_ref, part, tm_offset + 1)

    def moved(x, dim, forward):
        return pltpu.roll(x, 1 if forward else x.shape[dim] - 1, dim)

    diffusivity, sea = shared[0], shared[1]
    row_ids = lax.broadcasted_iota(jnp.int32, (height, width), 0)
    north_open, south_open = row_ids > 0, row_ids < height - 1
    north = 0.5 * (jnp.where(north_open, moved(diffusivity, 0, True), 0.0) + diffusivity)
    south = 0.5 * (diffusivity + jnp.where(south_open, moved(diffusivity, 0, False), 0.0))
    west = 0.5 * (moved(diffusivity, 1, True) + diffusivity)
    east = 0.5 * (diffusivity + moved(diffusivity, 1, False))
    coef[0] = jnp.where(north_open, north, 0.0)
    coef[1] = jnp.where(south_open, south, 0.0)
    coef[2] = west
    coef[3] = east
    coef[4] = north + south + west + east

    def operate(field, span, use):
        sea = shared[1]
        for t in range(n_tm):
            masked = [[field[s, v] * sea for v in range(variables)] for s in range(n_tm)]
            centre = (diag[t] + coef[4])[:, :span]
            for v in range(variables):
                here = masked[t][v]
                mixed = centre * here[:, :span]
                for w in range(variables):
                    mixed = mixed + factors_ref[v * variables + w, :, :span] * masked[t][w][:, :span]
                for s in range(n_tm):
                    mixed = mixed + factors_ref[variables * variables + t * n_tm + s, :, :span] * masked[s][v][:, :span]
                spread = (
                    coef[0, :, :span] * moved(here[:, :span], 0, True)
                    + coef[1, :, :span] * moved(here[:, :span], 0, False)
                    + coef[2, :, :span] * moved(here, 1, True)[:, :span]
                    + coef[3, :, :span] * moved(here, 1, False)[:, :span]
                )
                use(t, v, sea[:, :span] * (mixed - spread) + (1.0 - sea[:, :span]) * field[t, v, :, :span])

    def sum_of(products):
        return jnp.sum(jnp.sum(products, axis=1, keepdims=True), axis=0, keepdims=True)

    fields = [(t, v) for t in range(n_tm) for v in range(variables)]
    none = jnp.zeros((height, cols), jnp.float32)
    bb, bw, ww, uu, ub, us, cross = [none] * 7
    for t, v in fields:
        start = sea * right[t, v]
        right[t, v] = start
        bb = bb + start[:, :cols] * start[:, :cols]

    def first_image(t, v, result):
        nonlocal bw, ww
        image[t, v] = result
        here = result[:, :cols]
        bw = bw + right[t, v, :, :cols] * here
        ww = ww + here * here

    operate(right, width, first_image)
    bb, ww = sum_of(bb), sum_of(ww)
    usable = (bb > 0.0) & (ww > 0.0)
    alpha = jnp.where(usable, jnp.sqrt(bb / jnp.where(usable, ww, 1.0)), 1.0)
    for t, v in fields:
        start = right[t, v]
        left = start - alpha * image[t, v]
        change[t, v] = left
        left, start = left[:, :cols], start[:, :cols]
        uu = uu + left * left
        ub = ub + left * start

    def second_image(t, v, result):
        nonlocal us, cross
        left, start = change[t, v, :, :cols], right[t, v, :, :cols]
        us = us + left * result
        cross = cross + (left * image[t, v, :, :cols] + start * result)
        image[t, v, :, cols:] = result

    operate(change, cols, second_image)
    own_rows = pl.ds(pl.multiple_of(lat * rows, rows), rows)
    for v in range(variables):
        own_ref[0, v] = right[tm, v, own_rows, :cols]
        own_ref[1, v] = image[tm, v, own_rows, :cols]
        own_ref[2, v] = change[tm, v, own_rows, :cols]
        own_ref[3, v] = image[tm, v, own_rows, cols:]
    for k, value in enumerate((alpha, bb, sum_of(bw), sum_of(uu), sum_of(ub), sum_of(us), sum_of(cross))):
        sums_ref[0, k : k + 1] = jnp.broadcast_to(value, (1, cols))
    sums_ref[0, 7:8] = jnp.zeros((1, cols), jnp.float32)


def update_kernel(own_ref, mine_ref, near_ref, far_ref, solution_ref, residual_ref):
    devices = [near_ref[k] for k in range(near_ref.shape[0])] + [far_ref[k] for k in range(far_ref.shape[0])]

    def over(values):
        return functools.reduce(jnp.add, values)

    def sums(device):
        return [device[k : k + 1] for k in range(7)]

    norm_start = over([sums(d)[1] for d in devices])
    step_first = norm_start / over([sums(d)[2] for d in devices])
    squares = []
    for d in devices:
        alpha, bb, bw, uu, ub, us, cross = sums(d)
        rho = step_first / alpha
        squares.append(rho * rho * uu + 2.0 * rho * (1.0 - rho) * ub + (1.0 - rho) * (1.0 - rho) * bb)
    norm_next = over(squares)
    share = norm_next / norm_start
    products = []
    for d in devices:
        alpha, bb, bw, uu, ub, us, cross = sums(d)
        rho = step_first / alpha
        kappa = 1.0 - rho + share
        products.append(rho * rho * us + rho * kappa * cross + kappa * kappa * bw)
    step_second = norm_next / over(products)
    rho = step_first / mine_ref[0, 0:1]
    kappa = 1.0 - rho + share
    for v in range(own_ref.shape[1]):
        start, image, left, left_image = (own_ref[k, v] for k in range(4))
        solution_ref[0, v, 0] = step_first * start + step_second * (rho * left + kappa * start)
        residual_ref[0, v, 0] = rho * left + (1.0 - rho) * start - step_second * (rho * left_image + kappa * image)


def bits(count):
    return [1 << k for k in range(count.bit_length() - 1)]


def swapped(x, axis, bit):
    return lax.ppermute(x, axis, [(i, i ^ bit) for i in range(lax.axis_size(axis))])


def gathered(x, axis):
    near, offsets = x[None], [0]
    for bit in reversed(bits(lax.axis_size(axis))[1:]):
        near = jnp.concatenate([near, swapped(near, axis, bit)], axis=0)
        offsets = offsets + [j + bit for j in offsets]
    return near, swapped(near, axis, 1), offsets


def per_device(class_ids, coef_table, land_mask, cross_cov, time_metric, obs_values, obs_weight, obs_cells, obs_count, block_owner):
    n_lat, n_lon, n_tm = (lax.axis_size(axis) for axis in ("lat", "lon", "tm"))
    rows, cols = class_ids.shape[1:]
    variables = obs_values.shape[1]
    stats = variables + 1
    vmem = pl.BlockSpec(memory_space=pltpu.VMEM)
    height = n_lat * rows
    half = jax.ShapeDtypeStruct((n_lon // 2, stats * n_lat + SIDES * height // cols, rows, cols), jnp.float32)
    values = obs_values.transpose(1, 0, 2)
    arguments = (block_owner[:, 0], obs_count, coef_table, cross_cov, time_metric, values, obs_weight, obs_cells, class_ids, land_mask)
    places = [pltpu.SMEM] * 5 + [pltpu.VMEM] * 5
    keep, send, planes, factors = pl.pallas_call(
        tile_kernel,
        out_shape=(
            half,
            half,
            jax.ShapeDtypeStruct((1, rows, cols), jnp.float32),
            jax.ShapeDtypeStruct((variables * variables + n_tm * n_tm, 1, 2 * cols), jnp.float32),
        ),
        in_specs=[pl.BlockSpec(memory_space=pltpu.HBM)] * INPUTS,
        out_specs=(vmem,) * 4,
        scratch_shapes=[
            pltpu.VMEM((n_lon, n_lat, stats, rows, cols), jnp.float32),
            pltpu.VMEM((n_lon, rows, SIDES * height), jnp.float32),
            *[place(x.shape, x.dtype) for place, x in zip(places, arguments)],
            pltpu.SemaphoreType.DMA((INPUTS,)),
        ],
        compiler_params=pltpu.CompilerParams(vmem_limit_bytes=32 * 1024 * 1024),
    )(*[pltpu.with_memory_space_constraint(x, pltpu.HBM) for x in arguments])

    partial = keep + swapped(send, "lon", 1)
    for bit in bits(n_lon)[1:]:
        partial = partial[0::2] + swapped(partial[1::2], "lon", bit)
    summed, lat_offsets = partial[0], [0]
    count = summed.shape[0]
    for bit in bits(n_lat):
        given = swapped(jnp.concatenate([summed, planes], axis=0), "lat", bit)
        summed = summed + given[:count]
        planes = jnp.concatenate([planes, given[count:]], axis=0)
        lat_offsets = lat_offsets + [i + bit for i in lat_offsets]
    strip = jnp.concatenate([summed, planes], axis=0)

    near, far, offsets = gathered(strip, "tm")
    field = pltpu.VMEM((n_tm, variables, height, 2 * cols), jnp.float32)
    plane = pltpu.VMEM((n_tm, height, 2 * cols), jnp.float32)
    own, sums = pl.pallas_call(
        functools.partial(strip_kernel, offsets, lat_offsets),
        out_shape=(
            jax.ShapeDtypeStruct((4, variables, rows, cols), jnp.float32),
            jax.ShapeDtypeStruct((1, rows, cols), jnp.float32),
        ),
        in_specs=[vmem] * 3,
        out_specs=(vmem, vmem),
        scratch_shapes=[field, field, field, plane, pltpu.VMEM((5, height, 2 * cols), jnp.float32), plane],
        compiler_params=pltpu.CompilerParams(vmem_limit_bytes=24 * 1024 * 1024),
    )(factors, near, far)

    near, far, _ = gathered(sums[0], "lon")
    out = jax.ShapeDtypeStruct((1, variables, 1, rows, cols), jnp.float32)
    return pl.pallas_call(
        update_kernel,
        out_shape=(out, out),
        in_specs=[vmem] * 4,
        out_specs=(vmem, vmem),
        compiler_params=pltpu.CompilerParams(vmem_limit_bytes=8 * 1024 * 1024),
    )(own, sums, near, far)


def solution(mesh):
    in_specs = (
        P(None, "lat", "lon"),
        P(),
        P(None, "lat", "lon"),
        P(),
        P(),
        P(ALL, None, None),
        P(ALL, None),
        P(ALL, None),
        P(ALL),
        P(ALL, None),
    )
    out_specs = (P("tm", None, None, "lat", "lon"), P("tm", None, None, "lat", "lon"))
    return jax.shard_map(per_device, mesh=mesh, in_specs=in_specs, out_specs=out_specs, check_vma=False)
```

```python
import functools

import jax
import jax.numpy as jnp
from jax import lax
from jax.experimental import pallas as pl
from jax.experimental.pallas import tpu as pltpu
from jax.sharding import PartitionSpec as P

GROUP = 64
SIDES = 4
INPUTS = 10
ALL = ("lat", "lon", "tm")


def exact_dot(x, ones):
    high = x.astype(jnp.bfloat16)
    rest = x - high.astype(jnp.float32)
    middle = rest.astype(jnp.bfloat16)
    low = (rest - middle.astype(jnp.float32)).astype(jnp.bfloat16)
    parts = jnp.dot(jnp.concatenate([high, middle, low], axis=0), ones, preferred_element_type=jnp.float32)
    count = x.shape[0]
    return parts[:count] + (parts[count : 2 * count] + parts[2 * count :])


def side_column(side, cols):
    return jnp.where(side < 2, side, side + cols - SIDES)


def edge_columns(height, cols):
    column = lax.broadcasted_iota(jnp.int32, (cols, SIDES * height), 0)
    side = lax.broadcasted_iota(jnp.int32, (cols, SIDES * height), 1) // height
    return jnp.where(column == side_column(side, cols), 1.0, 0.0).astype(jnp.bfloat16)


def tile_kernel(*refs):
    arguments, (keep_ref, send_ref, plane_ref, factors_ref, tiles, packed) = refs[:INPUTS], refs[INPUTS : INPUTS + 6]
    local, arrived = refs[INPUTS + 6 : -1], refs[-1]
    owner_ref, count_ref, table_ref, cov_ref, metric_ref, values_ref, weight_ref, cells_ref, class_ref, land_ref = local
    copies = [pltpu.make_async_copy(a, b, arrived.at[k]) for k, (a, b) in enumerate(zip(arguments, local))]
    for copy in copies:
        copy.start()
    tiles[...] = jnp.zeros_like(tiles)
    variables, block_total, slots = values_ref.shape
    n_lon, n_lat, stats, rows, cols = tiles.shape
    lat, lon, tm = lax.axis_index("lat"), lax.axis_index("lon"), lax.axis_index("tm")
    for copy in copies:
        copy.wait()

    diffusivity = jnp.zeros((rows, cols), jnp.float32)
    for index in range(table_ref.shape[0]):
        diffusivity = jnp.where(class_ref[0] == index, table_ref[index], diffusivity)
    sea = land_ref[0].astype(jnp.float32)
    plane = jnp.where(tm == 0, diffusivity, sea)
    plane_ref[0] = plane
    months = metric_ref.shape[0]
    for v in range(variables):
        for w in range(variables):
            factors_ref[v * variables + w] = jnp.full(factors_ref.shape[1:], cov_ref[v, w])
    for t in range(months):
        for u in range(months):
            factors_ref[variables * variables + t * months + u] = jnp.full(factors_ref.shape[1:], metric_ref[t, u])

    lane = lax.broadcasted_iota(jnp.int32, (1, slots), 1)
    row_ids = lax.broadcasted_iota(jnp.int32, (rows, slots), 0)
    col_ids = lax.broadcasted_iota(jnp.int32, (cols, slots), 0).astype(jnp.int16)
    one, zero = jnp.ones((cols, slots), jnp.bfloat16), jnp.zeros((cols, slots), jnp.bfloat16)

    nothing = jnp.zeros((2 * stats * rows, slots), jnp.bfloat16)

    def operands(block):
        live = jnp.where(lane < count_ref[block], weight_ref[pl.ds(block, 1), :], 0.0)
        cells = cells_ref[pl.ds(block, 1), :]
        row_hit = row_ids == cells // cols
        terms = [live] + [live * values_ref[v, pl.ds(block, 1), :] for v in range(variables)]
        high = [term.astype(jnp.bfloat16).astype(jnp.float32) for term in terms]
        low = [term - part for term, part in zip(terms, high)]
        spread = jnp.concatenate([jnp.where(row_hit, part, 0.0) for part in high + low], axis=0)
        at_col = jnp.broadcast_to((cells % cols).astype(jnp.int16), (cols, slots))
        return spread.astype(jnp.bfloat16), jnp.where(at_col == col_ids, one, zero)

    def pair_sums(block):
        (first, first_hot), (second, second_hot) = operands(block), operands(block + 1)
        both = lax.dot_general(
            jnp.concatenate([jnp.concatenate([first, nothing], axis=1), jnp.concatenate([nothing, second], axis=1)], axis=0),
            jnp.concatenate([first_hot, second_hot], axis=1),
            (((1,), (1,)), ((), ())),
            preferred_element_type=jnp.float32,
        ).reshape(2, 2, stats, rows, cols)
        return [both[0, 0] + both[0, 1], both[1, 0] + both[1, 1]]

    def step(group, carry):
        sums = []
        for k in range(0, GROUP, 2):
            sums += pair_sums(group * GROUP + k)
        for k in range(GROUP):
            owner = owner_ref[group * GROUP + k]
            tiles[jnp.bitwise_xor(owner % n_lon, lon), owner // n_lon] += sums[k]
        return carry

    lax.fori_loop(0, block_total // GROUP, step, 0)
    own_tiles = stats * n_lat
    for m in range(n_lon // 2):
        for i in range(n_lat):
            for s in range(stats):
                keep_ref[m, s * n_lat + i] = tiles[2 * m, i, s]
                send_ref[m, s * n_lat + i] = tiles[2 * m + 1, i, s]

    height = n_lat * rows
    lanes = SIDES * height
    edges = edge_columns(height, cols)
    row = lax.broadcasted_iota(jnp.int32, (height, lanes), 0)
    at_row = lax.broadcasted_iota(jnp.int32, (height, lanes), 1) % height == row
    own_row = lax.broadcasted_iota(jnp.int32, (rows, lanes), 1) % height == lax.broadcasted_iota(jnp.int32, (rows, lanes), 0) + lat * rows
    blank = jnp.zeros((1, lanes), jnp.float32)
    for offset in range(n_lon):
        picked = exact_dot(jnp.concatenate([tiles[offset, i, s] for s in range(stats) for i in range(n_lat)], axis=0), edges)
        rows_of = [jnp.where(at_row, picked[s * height : (s + 1) * height], 0.0) for s in range(stats)]
        rows_of.append(jnp.where(own_row, exact_dot(plane, edges), 0.0) if offset == 0 else blank)
        sums = [jnp.sum(x, axis=0, keepdims=True) for x in rows_of]
        packed[offset] = jnp.concatenate(sums + [blank] * (rows - stats - 1), axis=0)
    from_after = lax.broadcasted_iota(jnp.int32, (rows, lanes), 1) < 2 * height
    for offset in range(n_lon):
        target = jnp.bitwise_xor(lon, offset)
        after = jnp.bitwise_xor(lon, lax.rem(target + 1, n_lon))
        before = jnp.bitwise_xor(lon, lax.rem(target + n_lon - 1, n_lon))
        beside = jnp.where(from_after, packed[after], packed[before])
        out_ref = send_ref if offset % 2 else keep_ref
        for c in range(lanes // cols):
            out_ref[offset // 2, own_tiles + c] = beside[:, c * cols : (c + 1) * cols]


def strip_kernel(offsets, lat_offsets, factors_ref, near_ref, far_ref, own_ref, sums_ref, right, image, change, diag, coef, shared):
    rows, cols = near_ref.shape[2:]
    n_tm, variables, height, width = right.shape
    stats, n_lat, lanes = variables + 1, height // rows, SIDES * height
    lat, tm = lax.axis_index("lat"), lax.axis_index("tm")
    chunks = lanes // cols
    first = stats * n_lat
    lane = lax.broadcasted_iota(jnp.int32, (height, lanes), 1)
    at_row = lane % height == lax.broadcasted_iota(jnp.int32, (height, lanes), 0)
    side = lax.broadcasted_iota(jnp.int32, (lanes, cols), 0) // height
    column = lax.broadcasted_iota(jnp.int32, (lanes, cols), 1)
    targets = jnp.where(column == side_column(side, cols), 1.0, 0.0).astype(jnp.bfloat16)

    def place(part_ref, part, tm_offset):
        t = jnp.bitwise_xor(tm, tm_offset)
        for i in range(n_lat):
            down = slice(i * rows, (i + 1) * rows)
            diag[t, down, :cols] = part_ref[part, i]
            for v in range(variables):
                right[t, v, down, :cols] = part_ref[part, (v + 1) * n_lat + i]

        for k, offset in enumerate(lat_offsets):
            down = pl.ds(pl.multiple_of(jnp.bitwise_xor(lat, offset) * rows, rows), rows)
            shared[t, down, :cols] = part_ref[part, first + chunks + k]

        beside = jnp.concatenate([part_ref[part, first + c] for c in range(chunks)], axis=1)
        spread = jnp.concatenate([jnp.where(at_row, beside[s : s + 1], 0.0) for s in range(stats + 1)], axis=0)
        columns = exact_dot(spread, targets)
        diag[t, :, cols:] = columns[:height]
        for v in range(variables):
            right[t, v, :, cols:] = columns[(v + 1) * height : (v + 2) * height]
        shared[t, :, cols:] = columns[stats * height :]

    for part, tm_offset in enumerate(offsets):
        place(near_ref, part, tm_offset)
        place(far_ref, part, tm_offset + 1)

    def moved(x, dim, forward):
        return pltpu.roll(x, 1 if forward else x.shape[dim] - 1, dim)

    diffusivity, sea = shared[0], shared[1]
    row_ids = lax.broadcasted_iota(jnp.int32, (height, width), 0)
    north_open, south_open = row_ids > 0, row_ids < height - 1
    north = 0.5 * (jnp.where(north_open, moved(diffusivity, 0, True), 0.0) + diffusivity)
    south = 0.5 * (diffusivity + jnp.where(south_open, moved(diffusivity, 0, False), 0.0))
    west = 0.5 * (moved(diffusivity, 1, True) + diffusivity)
    east = 0.5 * (diffusivity + moved(diffusivity, 1, False))
    coef[0] = jnp.where(north_open, north, 0.0)
    coef[1] = jnp.where(south_open, south, 0.0)
    coef[2] = west
    coef[3] = east
    coef[4] = north + south + west + east

    def operate(field, span, use):
        sea = shared[1]
        for t in range(n_tm):
            masked = [[field[s, v] * sea for v in range(variables)] for s in range(n_tm)]
            centre = (diag[t] + coef[4])[:, :span]
            for v in range(variables):
                here = masked[t][v]
                mixed = centre * here[:, :span]
                for w in range(variables):
                    mixed = mixed + factors_ref[v * variables + w, :, :span] * masked[t][w][:, :span]
                for s in range(n_tm):
                    mixed = mixed + factors_ref[variables * variables + t * n_tm + s, :, :span] * masked[s][v][:, :span]
                spread = (
                    coef[0, :, :span] * moved(here[:, :span], 0, True)
                    + coef[1, :, :span] * moved(here[:, :span], 0, False)
                    + coef[2, :, :span] * moved(here, 1, True)[:, :span]
                    + coef[3, :, :span] * moved(here, 1, False)[:, :span]
                )
                use(t, v, sea[:, :span] * (mixed - spread) + (1.0 - sea[:, :span]) * field[t, v, :, :span])

    def sum_of(products):
        return jnp.sum(jnp.sum(products, axis=1, keepdims=True), axis=0, keepdims=True)

    fields = [(t, v) for t in range(n_tm) for v in range(variables)]
    none = jnp.zeros((height, cols), jnp.float32)
    bb, bw, ww, uu, ub, us, cross = [none] * 7
    for t, v in fields:
        start = sea * right[t, v]
        right[t, v] = start
        bb = bb + start[:, :cols] * start[:, :cols]

    def first_image(t, v, result):
        nonlocal bw, ww
        image[t, v] = result
        here = result[:, :cols]
        bw = bw + right[t, v, :, :cols] * here
        ww = ww + here * here

    operate(right, width, first_image)
    bb, ww = sum_of(bb), sum_of(ww)
    usable = (bb > 0.0) & (ww > 0.0)
    alpha = jnp.where(usable, jnp.sqrt(bb / jnp.where(usable, ww, 1.0)), 1.0)
    for t, v in fields:
        start = right[t, v]
        left = start - alpha * image[t, v]
        change[t, v] = left
        left, start = left[:, :cols], start[:, :cols]
        uu = uu + left * left
        ub = ub + left * start

    def second_image(t, v, result):
        nonlocal us, cross
        left, start = change[t, v, :, :cols], right[t, v, :, :cols]
        us = us + left * result
        cross = cross + (left * image[t, v, :, :cols] + start * result)
        image[t, v, :, cols:] = result

    operate(change, cols, second_image)
    own_rows = pl.ds(pl.multiple_of(lat * rows, rows), rows)
    for v in range(variables):
        own_ref[0, v] = right[tm, v, own_rows, :cols]
        own_ref[1, v] = image[tm, v, own_rows, :cols]
        own_ref[2, v] = change[tm, v, own_rows, :cols]
        own_ref[3, v] = image[tm, v, own_rows, cols:]
    for k, value in enumerate((alpha, bb, sum_of(bw), sum_of(uu), sum_of(ub), sum_of(us), sum_of(cross))):
        sums_ref[0, k : k + 1] = jnp.broadcast_to(value, (1, cols))
    sums_ref[0, 7:8] = jnp.zeros((1, cols), jnp.float32)


def update_kernel(own_ref, mine_ref, near_ref, far_ref, solution_ref, residual_ref):
    devices = [near_ref[k] for k in range(near_ref.shape[0])] + [far_ref[k] for k in range(far_ref.shape[0])]

    def over(values):
        return functools.reduce(jnp.add, values)

    def sums(device):
        return [device[k : k + 1] for k in range(7)]

    norm_start = over([sums(d)[1] for d in devices])
    step_first = norm_start / over([sums(d)[2] for d in devices])
    squares = []
    for d in devices:
        alpha, bb, bw, uu, ub, us, cross = sums(d)
        rho = step_first / alpha
        squares.append(rho * rho * uu + 2.0 * rho * (1.0 - rho) * ub + (1.0 - rho) * (1.0 - rho) * bb)
    norm_next = over(squares)
    share = norm_next / norm_start
    products = []
    for d in devices:
        alpha, bb, bw, uu, ub, us, cross = sums(d)
        rho = step_first / alpha
        kappa = 1.0 - rho + share
        products.append(rho * rho * us + rho * kappa * cross + kappa * kappa * bw)
    step_second = norm_next / over(products)
    rho = step_first / mine_ref[0, 0:1]
    kappa = 1.0 - rho + share
    for v in range(own_ref.shape[1]):
        start, image, left, left_image = (own_ref[k, v] for k in range(4))
        solution_ref[0, v, 0] = step_first * start + step_second * (rho * left + kappa * start)
        residual_ref[0, v, 0] = rho * left + (1.0 - rho) * start - step_second * (rho * left_image + kappa * image)


def bits(count):
    return [1 << k for k in range(count.bit_length() - 1)]


def swapped(x, axis, bit):
    return lax.ppermute(x, axis, [(i, i ^ bit) for i in range(lax.axis_size(axis))])


def gathered(x, axis):
    near, offsets = x[None], [0]
    for bit in reversed(bits(lax.axis_size(axis))[1:]):
        near = jnp.concatenate([near, swapped(near, axis, bit)], axis=0)
        offsets = offsets + [j + bit for j in offsets]
    return near, swapped(near, axis, 1), offsets


def per_device(class_ids, coef_table, land_mask, cross_cov, time_metric, obs_values, obs_weight, obs_cells, obs_count, block_owner):
    n_lat, n_lon, n_tm = (lax.axis_size(axis) for axis in ("lat", "lon", "tm"))
    rows, cols = class_ids.shape[1:]
    variables = obs_values.shape[1]
    stats = variables + 1
    vmem = pl.BlockSpec(memory_space=pltpu.VMEM)
    height = n_lat * rows
    half = jax.ShapeDtypeStruct((n_lon // 2, stats * n_lat + SIDES * height // cols, rows, cols), jnp.float32)
    values = obs_values.transpose(1, 0, 2)
    arguments = (block_owner[:, 0], obs_count, coef_table, cross_cov, time_metric, values, obs_weight, obs_cells, class_ids, land_mask)
    places = [pltpu.SMEM] * 5 + [pltpu.VMEM] * 5
    keep, send, planes, factors = pl.pallas_call(
        tile_kernel,
        out_shape=(
            half,
            half,
            jax.ShapeDtypeStruct((1, rows, cols), jnp.float32),
            jax.ShapeDtypeStruct((variables * variables + n_tm * n_tm, 1, 2 * cols), jnp.float32),
        ),
        in_specs=[pl.BlockSpec(memory_space=pltpu.HBM)] * INPUTS,
        out_specs=(vmem,) * 4,
        scratch_shapes=[
            pltpu.VMEM((n_lon, n_lat, stats, rows, cols), jnp.float32),
            pltpu.VMEM((n_lon, rows, SIDES * height), jnp.float32),
            *[place(x.shape, x.dtype) for place, x in zip(places, arguments)],
            pltpu.SemaphoreType.DMA((INPUTS,)),
        ],
        compiler_params=pltpu.CompilerParams(vmem_limit_bytes=32 * 1024 * 1024),
    )(*[pltpu.with_memory_space_constraint(x, pltpu.HBM) for x in arguments])

    partial = keep + swapped(send, "lon", 1)
    for bit in bits(n_lon)[1:]:
        partial = partial[0::2] + swapped(partial[1::2], "lon", bit)
    summed, lat_offsets = partial[0], [0]
    count = summed.shape[0]
    for bit in bits(n_lat):
        given = swapped(jnp.concatenate([summed, planes], axis=0), "lat", bit)
        summed = summed + given[:count]
        planes = jnp.concatenate([planes, given[count:]], axis=0)
        lat_offsets = lat_offsets + [i + bit for i in lat_offsets]
    strip = jnp.concatenate([summed, planes], axis=0)

    near, far, offsets = gathered(strip, "tm")
    field = pltpu.VMEM((n_tm, variables, height, 2 * cols), jnp.float32)
    plane = pltpu.VMEM((n_tm, height, 2 * cols), jnp.float32)
    own, sums = pl.pallas_call(
        functools.partial(strip_kernel, offsets, lat_offsets),
        out_shape=(
            jax.ShapeDtypeStruct((4, variables, rows, cols), jnp.float32),
            jax.ShapeDtypeStruct((1, rows, cols), jnp.float32),
        ),
        in_specs=[vmem] * 3,
        out_specs=(vmem, vmem),
        scratch_shapes=[field, field, field, plane, pltpu.VMEM((5, height, 2 * cols), jnp.float32), plane],
        compiler_params=pltpu.CompilerParams(vmem_limit_bytes=24 * 1024 * 1024),
    )(factors, near, far)

    near, far, _ = gathered(sums[0], "lon")
    out = jax.ShapeDtypeStruct((1, variables, 1, rows, cols), jnp.float32)
    return pl.pallas_call(
        update_kernel,
        out_shape=(out, out),
        in_specs=[vmem] * 4,
        out_specs=(vmem, vmem),
        compiler_params=pltpu.CompilerParams(vmem_limit_bytes=8 * 1024 * 1024),
    )(own, sums, near, far)


def solution(mesh):
    in_specs = (
        P(None, "lat", "lon"),
        P(),
        P(None, "lat", "lon"),
        P(),
        P(),
        P(ALL, None, None),
        P(ALL, None),
        P(ALL, None),
        P(ALL),
        P(ALL, None),
    )
    out_specs = (P("tm", None, None, "lat", "lon"), P("tm", None, None, "lat", "lon"))
    return jax.shard_map(per_device, mesh=mesh, in_specs=in_specs, out_specs=out_specs, check_vma=False)
```

```python
import functools

import jax
import jax.numpy as jnp
from jax import lax
from jax.experimental import pallas as pl
from jax.experimental.pallas import tpu as pltpu
from jax.sharding import PartitionSpec as P

GROUP = 8
SIDES = 4
INPUTS = 10
ALL = ("lat", "lon", "tm")


def exact_dot(x, ones):
    high = x.astype(jnp.bfloat16)
    rest = x - high.astype(jnp.float32)
    middle = rest.astype(jnp.bfloat16)
    low = (rest - middle.astype(jnp.float32)).astype(jnp.bfloat16)
    parts = jnp.dot(jnp.concatenate([high, middle, low], axis=0), ones, preferred_element_type=jnp.float32)
    count = x.shape[0]
    return parts[:count] + (parts[count : 2 * count] + parts[2 * count :])


def side_column(side, cols):
    return jnp.where(side < 2, side, side + cols - SIDES)


def edge_columns(height, cols):
    column = lax.broadcasted_iota(jnp.int32, (cols, SIDES * height), 0)
    side = lax.broadcasted_iota(jnp.int32, (cols, SIDES * height), 1) // height
    return jnp.where(column == side_column(side, cols), 1.0, 0.0).astype(jnp.bfloat16)


def tile_kernel(*refs):
    arguments, (keep_ref, send_ref, plane_ref, factors_ref, tiles, packed) = refs[:INPUTS], refs[INPUTS : INPUTS + 6]
    local, arrived = refs[INPUTS + 6 : -1], refs[-1]
    owner_ref, count_ref, table_ref, cov_ref, metric_ref, values_ref, weight_ref, cells_ref, class_ref, land_ref = local
    copies = [pltpu.make_async_copy(a, b, arrived.at[k]) for k, (a, b) in enumerate(zip(arguments, local))]
    for copy in copies[5:8] + copies[:5] + copies[8:]:
        copy.start()
    tiles[...] = jnp.zeros_like(tiles)
    variables, block_total, slots = values_ref.shape
    n_lon, n_lat, stats, rows, cols = tiles.shape
    lat, lon, tm = lax.axis_index("lat"), lax.axis_index("lon"), lax.axis_index("tm")
    for copy in copies:
        copy.wait()

    diffusivity = jnp.zeros((rows, cols), jnp.float32)
    for index in range(table_ref.shape[0]):
        diffusivity = jnp.where(class_ref[0] == index, table_ref[index], diffusivity)
    sea = land_ref[0].astype(jnp.float32)
    plane = jnp.where(tm == 0, diffusivity, sea)
    plane_ref[0] = plane
    months = metric_ref.shape[0]
    for v in range(variables):
        for w in range(variables):
            factors_ref[v * variables + w] = jnp.full(factors_ref.shape[1:], cov_ref[v, w])
    for t in range(months):
        for u in range(months):
            factors_ref[variables * variables + t * months + u] = jnp.full(factors_ref.shape[1:], metric_ref[t, u])

    lane = lax.broadcasted_iota(jnp.int32, (GROUP, slots), 1)
    turn = lax.broadcasted_iota(jnp.int32, (GROUP, slots), 0)
    row_ids = lax.broadcasted_iota(jnp.int32, (rows, slots), 0)
    col_ids = lax.broadcasted_iota(jnp.int32, (cols, slots), 0).astype(jnp.int16)
    one, zero = jnp.ones((cols, slots), jnp.bfloat16), jnp.zeros((cols, slots), jnp.bfloat16)
    nothing = jnp.zeros((2 * stats * rows, slots), jnp.bfloat16)

    def pair_sums(parts, row_of, col_of, k):
        spread, hot = [], []
        for at in (slice(k, k + 1), slice(k + 1, k + 2)):
            row_hit = row_ids == row_of[at]
            spread.append(jnp.concatenate([jnp.where(row_hit, part[at], 0.0) for part in parts], axis=0).astype(jnp.bfloat16))
            hot.append(jnp.where(jnp.broadcast_to(col_of[at].astype(jnp.int16), (cols, slots)) == col_ids, one, zero))
        both = lax.dot_general(
            jnp.concatenate([jnp.concatenate([spread[0], nothing], axis=1), jnp.concatenate([nothing, spread[1]], axis=1)], axis=0),
            jnp.concatenate(hot, axis=1),
            (((1,), (1,)), ((), ())),
            preferred_element_type=jnp.float32,
        ).reshape(2, 2, stats, rows, cols)
        return [both[0, 0] + both[0, 1], both[1, 0] + both[1, 1]]

    sums = []
    for first in range(0, block_total, GROUP):
        blocks = slice(first, first + GROUP)
        counts = jnp.zeros((GROUP, slots), jnp.int32)
        for k in range(GROUP):
            counts = jnp.where(turn == k, count_ref[first + k], counts)
        live = jnp.where(lane < counts, weight_ref[blocks], 0.0)
        terms = [live] + [live * values_ref[v, blocks] for v in range(variables)]
        high = [term.astype(jnp.bfloat16).astype(jnp.float32) for term in terms]
        low = [term - part for term, part in zip(terms, high)]
        row_of, col_of = cells_ref[blocks] // cols, cells_ref[blocks] % cols
        for k in range(0, GROUP, 2):
            sums += pair_sums(high + low, row_of, col_of, k)
    for block in range(block_total):
        owner = owner_ref[block]
        tiles[jnp.bitwise_xor(owner % n_lon, lon), owner // n_lon] += sums[block]
    own_tiles = stats * n_lat
    for m in range(n_lon // 2):
        for i in range(n_lat):
            for s in range(stats):
                keep_ref[m, s * n_lat + i] = tiles[2 * m, i, s]
                send_ref[m, s * n_lat + i] = tiles[2 * m + 1, i, s]

    height = n_lat * rows
    lanes = SIDES * height
    edges = edge_columns(height, cols)
    row = lax.broadcasted_iota(jnp.int32, (height, lanes), 0)
    at_row = lax.broadcasted_iota(jnp.int32, (height, lanes), 1) % height == row
    own_row = lax.broadcasted_iota(jnp.int32, (rows, lanes), 1) % height == lax.broadcasted_iota(jnp.int32, (rows, lanes), 0) + lat * rows
    blank = jnp.zeros((1, lanes), jnp.float32)
    stacked = [tiles[offset, i, s] for offset in range(n_lon) for s in range(stats) for i in range(n_lat)]
    picked = exact_dot(jnp.concatenate(stacked + [plane], axis=0), edges)
    tall = stats * height
    for offset in range(n_lon):
        rows_of = [jnp.where(at_row, picked[offset * tall + s * height : offset * tall + (s + 1) * height], 0.0) for s in range(stats)]
        rows_of.append(jnp.where(own_row, picked[n_lon * tall :], 0.0) if offset == 0 else blank)
        sums = [jnp.sum(x, axis=0, keepdims=True) for x in rows_of]
        packed[offset] = jnp.concatenate(sums + [blank] * (rows - stats - 1), axis=0)
    from_after = lax.broadcasted_iota(jnp.int32, (rows, lanes), 1) < 2 * height
    for offset in range(n_lon):
        target = jnp.bitwise_xor(lon, offset)
        after = jnp.bitwise_xor(lon, lax.rem(target + 1, n_lon))
        before = jnp.bitwise_xor(lon, lax.rem(target + n_lon - 1, n_lon))
        beside = jnp.where(from_after, packed[after], packed[before])
        out_ref = send_ref if offset % 2 else keep_ref
        for c in range(lanes // cols):
            out_ref[offset // 2, own_tiles + c] = beside[:, c * cols : (c + 1) * cols]


def strip_kernel(offsets, lat_offsets, factors_ref, near_ref, far_ref, own_ref, sums_ref, right, image, change, diag, coef, shared):
    rows, cols = near_ref.shape[2:]
    n_tm, variables, height, width = right.shape
    stats, n_lat, lanes = variables + 1, height // rows, SIDES * height
    lat, tm = lax.axis_index("lat"), lax.axis_index("tm")
    chunks = lanes // cols
    first = stats * n_lat
    lane = lax.broadcasted_iota(jnp.int32, (height, lanes), 1)
    at_row = lane % height == lax.broadcasted_iota(jnp.int32, (height, lanes), 0)
    side = lax.broadcasted_iota(jnp.int32, (lanes, cols), 0) // height
    column = lax.broadcasted_iota(jnp.int32, (lanes, cols), 1)
    targets = jnp.where(column == side_column(side, cols), 1.0, 0.0).astype(jnp.bfloat16)

    def place(part_ref, part, tm_offset):
        t = jnp.bitwise_xor(tm, tm_offset)
        for i in range(n_lat):
            down = slice(i * rows, (i + 1) * rows)
            diag[t, down, :cols] = part_ref[part, i]
            for v in range(variables):
                right[t, v, down, :cols] = part_ref[part, (v + 1) * n_lat + i]

        for k, offset in enumerate(lat_offsets):
            down = pl.ds(pl.multiple_of(jnp.bitwise_xor(lat, offset) * rows, rows), rows)
            shared[t, down, :cols] = part_ref[part, first + chunks + k]

        beside = jnp.concatenate([part_ref[part, first + c] for c in range(chunks)], axis=1)
        spread = jnp.concatenate([jnp.where(at_row, beside[s : s + 1], 0.0) for s in range(stats + 1)], axis=0)
        columns = exact_dot(spread, targets)
        diag[t, :, cols:] = columns[:height]
        for v in range(variables):
            right[t, v, :, cols:] = columns[(v + 1) * height : (v + 2) * height]
        shared[t, :, cols:] = columns[stats * height :]

    for part, tm_offset in enumerate(offsets):
        place(near_ref, part, tm_offset)
        place(far_ref, part, tm_offset + 1)

    def moved(x, dim, forward):
        return pltpu.roll(x, 1 if forward else x.shape[dim] - 1, dim)

    diffusivity, sea = shared[0], shared[1]
    row_ids = lax.broadcasted_iota(jnp.int32, (height, width), 0)
    north_open, south_open = row_ids > 0, row_ids < height - 1
    north = 0.5 * (jnp.where(north_open, moved(diffusivity, 0, True), 0.0) + diffusivity)
    south = 0.5 * (diffusivity + jnp.where(south_open, moved(diffusivity, 0, False), 0.0))
    west = 0.5 * (moved(diffusivity, 1, True) + diffusivity)
    east = 0.5 * (diffusivity + moved(diffusivity, 1, False))
    coef[0] = jnp.where(north_open, north, 0.0)
    coef[1] = jnp.where(south_open, south, 0.0)
    coef[2] = west
    coef[3] = east
    coef[4] = north + south + west + east

    def operate(field, span, use):
        sea = shared[1]
        for t in range(n_tm):
            masked = [[field[s, v] * sea for v in range(variables)] for s in range(n_tm)]
            centre = (diag[t] + coef[4])[:, :span]
            for v in range(variables):
                here = masked[t][v]
                mixed = centre * here[:, :span]
                for w in range(variables):
                    mixed = mixed + factors_ref[v * variables + w, :, :span] * masked[t][w][:, :span]
                for s in range(n_tm):
                    mixed = mixed + factors_ref[variables * variables + t * n_tm + s, :, :span] * masked[s][v][:, :span]
                spread = (
                    coef[0, :, :span] * moved(here[:, :span], 0, True)
                    + coef[1, :, :span] * moved(here[:, :span], 0, False)
                    + coef[2, :, :span] * moved(here, 1, True)[:, :span]
                    + coef[3, :, :span] * moved(here, 1, False)[:, :span]
                )
                use(t, v, sea[:, :span] * (mixed - spread) + (1.0 - sea[:, :span]) * field[t, v, :, :span])

    def sum_of(products):
        return jnp.sum(jnp.sum(products, axis=1, keepdims=True), axis=0, keepdims=True)

    fields = [(t, v) for t in range(n_tm) for v in range(variables)]
    none = jnp.zeros((height, cols), jnp.float32)
    bb, bw, ww, uu, ub, us, cross = [none] * 7
    for t, v in fields:
        start = sea * right[t, v]
        right[t, v] = start
        bb = bb + start[:, :cols] * start[:, :cols]

    def first_image(t, v, result):
        nonlocal bw, ww
        image[t, v] = result
        here = result[:, :cols]
        bw = bw + right[t, v, :, :cols] * here
        ww = ww + here * here

    operate(right, width, first_image)
    bb, ww = sum_of(bb), sum_of(ww)
    usable = (bb > 0.0) & (ww > 0.0)
    alpha = jnp.where(usable, jnp.sqrt(bb / jnp.where(usable, ww, 1.0)), 1.0)
    for t, v in fields:
        start = right[t, v]
        left = start - alpha * image[t, v]
        change[t, v] = left
        left, start = left[:, :cols], start[:, :cols]
        uu = uu + left * left
        ub = ub + left * start

    def second_image(t, v, result):
        nonlocal us, cross
        left, start = change[t, v, :, :cols], right[t, v, :, :cols]
        us = us + left * result
        cross = cross + (left * image[t, v, :, :cols] + start * result)
        image[t, v, :, cols:] = result

    operate(change, cols, second_image)
    own_rows = pl.ds(pl.multiple_of(lat * rows, rows), rows)
    for v in range(variables):
        own_ref[0, v] = right[tm, v, own_rows, :cols]
        own_ref[1, v] = image[tm, v, own_rows, :cols]
        own_ref[2, v] = change[tm, v, own_rows, :cols]
        own_ref[3, v] = image[tm, v, own_rows, cols:]
    for k, value in enumerate((alpha, bb, sum_of(bw), sum_of(uu), sum_of(ub), sum_of(us), sum_of(cross))):
        sums_ref[0, k : k + 1] = jnp.broadcast_to(value, (1, cols))
    sums_ref[0, 7:8] = jnp.zeros((1, cols), jnp.float32)


def update_kernel(own_ref, mine_ref, near_ref, far_ref, solution_ref, residual_ref):
    devices = [near_ref[k] for k in range(near_ref.shape[0])] + [far_ref[k] for k in range(far_ref.shape[0])]

    def over(values):
        return functools.reduce(jnp.add, values)

    def sums(device):
        return [device[k : k + 1] for k in range(7)]

    norm_start = over([sums(d)[1] for d in devices])
    step_first = norm_start / over([sums(d)[2] for d in devices])
    squares = []
    for d in devices:
        alpha, bb, bw, uu, ub, us, cross = sums(d)
        rho = step_first / alpha
        squares.append(rho * rho * uu + 2.0 * rho * (1.0 - rho) * ub + (1.0 - rho) * (1.0 - rho) * bb)
    norm_next = over(squares)
    share = norm_next / norm_start
    products = []
    for d in devices:
        alpha, bb, bw, uu, ub, us, cross = sums(d)
        rho = step_first / alpha
        kappa = 1.0 - rho + share
        products.append(rho * rho * us + rho * kappa * cross + kappa * kappa * bw)
    step_second = norm_next / over(products)
    rho = step_first / mine_ref[0, 0:1]
    kappa = 1.0 - rho + share
    for v in range(own_ref.shape[1]):
        start, image, left, left_image = (own_ref[k, v] for k in range(4))
        solution_ref[0, v, 0] = step_first * start + step_second * (rho * left + kappa * start)
        residual_ref[0, v, 0] = rho * left + (1.0 - rho) * start - step_second * (rho * left_image + kappa * image)


def bits(count):
    return [1 << k for k in range(count.bit_length() - 1)]


def swapped(x, axis, bit):
    return lax.ppermute(x, axis, [(i, i ^ bit) for i in range(lax.axis_size(axis))])


def gathered(x, axis):
    near, offsets = x[None], [0]
    for bit in reversed(bits(lax.axis_size(axis))[1:]):
        near = jnp.concatenate([near, swapped(near, axis, bit)], axis=0)
        offsets = offsets + [j + bit for j in offsets]
    return near, swapped(near, axis, 1), offsets


def per_device(class_ids, coef_table, land_mask, cross_cov, time_metric, obs_values, obs_weight, obs_cells, obs_count, block_owner):
    n_lat, n_lon, n_tm = (lax.axis_size(axis) for axis in ("lat", "lon", "tm"))
    rows, cols = class_ids.shape[1:]
    variables = obs_values.shape[1]
    stats = variables + 1
    vmem = pl.BlockSpec(memory_space=pltpu.VMEM)
    height = n_lat * rows
    half = jax.ShapeDtypeStruct((n_lon // 2, stats * n_lat + SIDES * height // cols, rows, cols), jnp.float32)
    values = obs_values.transpose(1, 0, 2)
    arguments = (block_owner[:, 0], obs_count, coef_table, cross_cov, time_metric, values, obs_weight, obs_cells, class_ids, land_mask)
    places = [pltpu.SMEM] * 5 + [pltpu.VMEM] * 5
    keep, send, planes, factors = pl.pallas_call(
        tile_kernel,
        out_shape=(
            half,
            half,
            jax.ShapeDtypeStruct((1, rows, cols), jnp.float32),
            jax.ShapeDtypeStruct((variables * variables + n_tm * n_tm, 1, 2 * cols), jnp.float32),
        ),
        in_specs=[pl.BlockSpec(memory_space=pltpu.HBM)] * INPUTS,
        out_specs=(vmem,) * 4,
        scratch_shapes=[
            pltpu.VMEM((n_lon, n_lat, stats, rows, cols), jnp.float32),
            pltpu.VMEM((n_lon, rows, SIDES * height), jnp.float32),
            *[place(x.shape, x.dtype) for place, x in zip(places, arguments)],
            pltpu.SemaphoreType.DMA((INPUTS,)),
        ],
        compiler_params=pltpu.CompilerParams(vmem_limit_bytes=32 * 1024 * 1024),
    )(*[pltpu.with_memory_space_constraint(x, pltpu.HBM) for x in arguments])

    partial = keep + swapped(send, "lon", 1)
    for bit in bits(n_lon)[1:]:
        partial = partial[0::2] + swapped(partial[1::2], "lon", bit)
    summed, lat_offsets = partial[0], [0]
    count = summed.shape[0]
    for bit in bits(n_lat):
        given = swapped(jnp.concatenate([summed, planes], axis=0), "lat", bit)
        summed = summed + given[:count]
        planes = jnp.concatenate([planes, given[count:]], axis=0)
        lat_offsets = lat_offsets + [i + bit for i in lat_offsets]
    strip = jnp.concatenate([summed, planes], axis=0)

    near, far, offsets = gathered(strip, "tm")
    field = pltpu.VMEM((n_tm, variables, height, 2 * cols), jnp.float32)
    plane = pltpu.VMEM((n_tm, height, 2 * cols), jnp.float32)
    own, sums = pl.pallas_call(
        functools.partial(strip_kernel, offsets, lat_offsets),
        out_shape=(
            jax.ShapeDtypeStruct((4, variables, rows, cols), jnp.float32),
            jax.ShapeDtypeStruct((1, rows, cols), jnp.float32),
        ),
        in_specs=[vmem] * 3,
        out_specs=(vmem, vmem),
        scratch_shapes=[field, field, field, plane, pltpu.VMEM((5, height, 2 * cols), jnp.float32), plane],
        compiler_params=pltpu.CompilerParams(vmem_limit_bytes=24 * 1024 * 1024),
    )(factors, near, far)

    near, far, _ = gathered(sums[0], "lon")
    out = jax.ShapeDtypeStruct((1, variables, 1, rows, cols), jnp.float32)
    return pl.pallas_call(
        update_kernel,
        out_shape=(out, out),
        in_specs=[vmem] * 4,
        out_specs=(vmem, vmem),
        compiler_params=pltpu.CompilerParams(vmem_limit_bytes=8 * 1024 * 1024),
    )(own, sums, near, far)


def solution(mesh):
    in_specs = (
        P(None, "lat", "lon"),
        P(),
        P(None, "lat", "lon"),
        P(),
        P(),
        P(ALL, None, None),
        P(ALL, None),
        P(ALL, None),
        P(ALL),
        P(ALL, None),
    )
    out_specs = (P("tm", None, None, "lat", "lon"), P("tm", None, None, "lat", "lon"))
    return jax.shard_map(per_device, mesh=mesh, in_specs=in_specs, out_specs=out_specs, check_vma=False)
```

```python
import functools

import jax
import jax.numpy as jnp
from jax import lax
from jax.experimental import pallas as pl
from jax.experimental.pallas import tpu as pltpu
from jax.sharding import PartitionSpec as P

GROUP = 8
SIDES = 4
INPUTS = 10
ALL = ("lat", "lon", "tm")


def exact_dot(x, ones):
    high = x.astype(jnp.bfloat16)
    rest = x - high.astype(jnp.float32)
    middle = rest.astype(jnp.bfloat16)
    low = (rest - middle.astype(jnp.float32)).astype(jnp.bfloat16)
    parts = jnp.dot(jnp.concatenate([high, middle, low], axis=0), ones, preferred_element_type=jnp.float32)
    count = x.shape[0]
    return parts[:count] + (parts[count : 2 * count] + parts[2 * count :])


def side_column(side, cols):
    return jnp.where(side < 2, side, side + cols - SIDES)


def edge_columns(height, cols):
    column = lax.broadcasted_iota(jnp.int32, (cols, SIDES * height), 0)
    side = lax.broadcasted_iota(jnp.int32, (cols, SIDES * height), 1) // height
    return jnp.where(column == side_column(side, cols), 1.0, 0.0).astype(jnp.bfloat16)


def tile_kernel(*refs):
    arguments, (keep_ref, send_ref, plane_ref, factors_ref, tiles, packed) = refs[:INPUTS], refs[INPUTS : INPUTS + 6]
    local, arrived = refs[INPUTS + 6 : -1], refs[-1]
    owner_ref, count_ref, table_ref, cov_ref, metric_ref, values_ref, weight_ref, cells_ref, class_ref, land_ref = local
    copies = [pltpu.make_async_copy(a, b, arrived.at[k]) for k, (a, b) in enumerate(zip(arguments, local))]
    for copy in copies[5:8] + copies[:5] + copies[8:]:
        copy.start()
    tiles[...] = jnp.zeros_like(tiles)
    variables, block_total, slots = values_ref.shape
    n_lon, n_lat, stats, rows, cols = tiles.shape
    lat, lon, tm = lax.axis_index("lat"), lax.axis_index("lon"), lax.axis_index("tm")
    for copy in copies:
        copy.wait()

    diffusivity = jnp.zeros((rows, cols), jnp.float32)
    for index in range(table_ref.shape[0]):
        diffusivity = jnp.where(class_ref[0] == index, table_ref[index], diffusivity)
    sea = land_ref[0].astype(jnp.float32)
    plane = jnp.where(tm == 0, diffusivity, sea)
    plane_ref[0] = plane
    months = metric_ref.shape[0]
    for v in range(variables):
        for w in range(variables):
            factors_ref[v * variables + w] = jnp.full(factors_ref.shape[1:], cov_ref[v, w])
    for t in range(months):
        for u in range(months):
            factors_ref[variables * variables + t * months + u] = jnp.full(factors_ref.shape[1:], metric_ref[t, u])

    lane = lax.broadcasted_iota(jnp.int32, (GROUP, slots), 1)
    turn = lax.broadcasted_iota(jnp.int32, (GROUP, slots), 0)
    row_ids = lax.broadcasted_iota(jnp.int32, (rows, slots), 0)
    col_ids = lax.broadcasted_iota(jnp.int32, (cols, slots), 0).astype(jnp.int16)
    one, zero = jnp.ones((cols, slots), jnp.bfloat16), jnp.zeros((cols, slots), jnp.bfloat16)
    nothing = jnp.zeros((2 * stats * rows, slots), jnp.bfloat16)

    def pair_sums(parts, row_of, col_of, k):
        spread, hot = [], []
        for at in (slice(k, k + 1), slice(k + 1, k + 2)):
            row_hit = row_ids == row_of[at]
            spread.append(jnp.concatenate([jnp.where(row_hit, part[at], 0.0) for part in parts], axis=0).astype(jnp.bfloat16))
            hot.append(jnp.where(jnp.broadcast_to(col_of[at].astype(jnp.int16), (cols, slots)) == col_ids, one, zero))
        both = lax.dot_general(
            jnp.concatenate([jnp.concatenate([spread[0], nothing], axis=1), jnp.concatenate([nothing, spread[1]], axis=1)], axis=0),
            jnp.concatenate(hot, axis=1),
            (((1,), (1,)), ((), ())),
            preferred_element_type=jnp.float32,
        ).reshape(2, 2, stats, rows, cols)
        return [both[0, 0] + both[0, 1], both[1, 0] + both[1, 1]]

    sums = []
    for first in range(0, block_total, GROUP):
        blocks = slice(first, first + GROUP)
        counts = jnp.zeros((GROUP, slots), jnp.int32)
        for k in range(GROUP):
            counts = jnp.where(turn == k, count_ref[first + k], counts)
        live = jnp.where(lane < counts, weight_ref[blocks], 0.0)
        terms = [live] + [live * values_ref[v, blocks] for v in range(variables)]
        high = [term.astype(jnp.bfloat16).astype(jnp.float32) for term in terms]
        low = [term - part for term, part in zip(terms, high)]
        row_of, col_of = cells_ref[blocks] // cols, cells_ref[blocks] % cols
        for k in range(0, GROUP, 2):
            sums += pair_sums(high + low, row_of, col_of, k)
    for block in range(block_total):
        owner = owner_ref[block]
        tiles[jnp.bitwise_xor(owner % n_lon, lon), owner // n_lon] += sums[block]
    own_tiles = stats * n_lat
    for m in range(n_lon // 2):
        for i in range(n_lat):
            for s in range(stats):
                keep_ref[m, s * n_lat + i] = tiles[2 * m, i, s]
                send_ref[m, s * n_lat + i] = tiles[2 * m + 1, i, s]

    height = n_lat * rows
    lanes = SIDES * height
    edges = edge_columns(height, cols)
    row = lax.broadcasted_iota(jnp.int32, (height, lanes), 0)
    at_row = lax.broadcasted_iota(jnp.int32, (height, lanes), 1) % height == row
    own_row = lax.broadcasted_iota(jnp.int32, (rows, lanes), 1) % height == lax.broadcasted_iota(jnp.int32, (rows, lanes), 0) + lat * rows
    blank = jnp.zeros((1, lanes), jnp.float32)
    stacked = [tiles[offset, i, s] for offset in range(n_lon) for s in range(stats) for i in range(n_lat)]
    picked = exact_dot(jnp.concatenate(stacked + [plane], axis=0), edges)
    tall = stats * height
    for offset in range(n_lon):
        rows_of = [jnp.where(at_row, picked[offset * tall + s * height : offset * tall + (s + 1) * height], 0.0) for s in range(stats)]
        rows_of.append(jnp.where(own_row, picked[n_lon * tall :], 0.0) if offset == 0 else blank)
        sums = [jnp.sum(x, axis=0, keepdims=True) for x in rows_of]
        packed[offset] = jnp.concatenate(sums + [blank] * (rows - stats - 1), axis=0)
    from_after = lax.broadcasted_iota(jnp.int32, (rows, lanes), 1) < 2 * height
    for offset in range(n_lon):
        target = jnp.bitwise_xor(lon, offset)
        after = jnp.bitwise_xor(lon, lax.rem(target + 1, n_lon))
        before = jnp.bitwise_xor(lon, lax.rem(target + n_lon - 1, n_lon))
        beside = jnp.where(from_after, packed[after], packed[before])
        out_ref = send_ref if offset % 2 else keep_ref
        for c in range(lanes // cols):
            out_ref[offset // 2, own_tiles + c] = beside[:, c * cols : (c + 1) * cols]


def strip_kernel(offsets, lat_offsets, factors_ref, near_ref, far_ref, own_ref, sums_ref, right, image, change, diag, coef, shared):
    rows, cols = near_ref.shape[2:]
    n_tm, variables, height, width = right.shape
    stats, n_lat, lanes = variables + 1, height // rows, SIDES * height
    lat, tm = lax.axis_index("lat"), lax.axis_index("tm")
    chunks = lanes // cols
    first = stats * n_lat
    lane = lax.broadcasted_iota(jnp.int32, (height, lanes), 1)
    at_row = lane % height == lax.broadcasted_iota(jnp.int32, (height, lanes), 0)
    side = lax.broadcasted_iota(jnp.int32, (lanes, cols), 0) // height
    column = lax.broadcasted_iota(jnp.int32, (lanes, cols), 1)
    targets = jnp.where(column == side_column(side, cols), 1.0, 0.0).astype(jnp.bfloat16)

    def place(part_ref, part, tm_offset):
        t = jnp.bitwise_xor(tm, tm_offset)
        for i in range(n_lat):
            down = slice(i * rows, (i + 1) * rows)
            diag[t, down, :cols] = part_ref[part, i]
            for v in range(variables):
                right[t, v, down, :cols] = part_ref[part, (v + 1) * n_lat + i]

        for k, offset in enumerate(lat_offsets):
            down = pl.ds(pl.multiple_of(jnp.bitwise_xor(lat, offset) * rows, rows), rows)
            shared[t, down, :cols] = part_ref[part, first + chunks + k]

        beside = jnp.concatenate([part_ref[part, first + c] for c in range(chunks)], axis=1)
        spread = jnp.concatenate([jnp.where(at_row, beside[s : s + 1], 0.0) for s in range(stats + 1)], axis=0)
        columns = exact_dot(spread, targets)
        diag[t, :, cols:] = columns[:height]
        for v in range(variables):
            right[t, v, :, cols:] = columns[(v + 1) * height : (v + 2) * height]
        shared[t, :, cols:] = columns[stats * height :]

    for part, tm_offset in enumerate(offsets):
        place(near_ref, part, tm_offset)
        place(far_ref, part, tm_offset + 1)

    def moved(x, dim, forward):
        return pltpu.roll(x, 1 if forward else x.shape[dim] - 1, dim)

    diffusivity, sea = shared[0], shared[1]
    row_ids = lax.broadcasted_iota(jnp.int32, (height, width), 0)
    north_open, south_open = row_ids > 0, row_ids < height - 1
    north = 0.5 * (jnp.where(north_open, moved(diffusivity, 0, True), 0.0) + diffusivity)
    south = 0.5 * (diffusivity + jnp.where(south_open, moved(diffusivity, 0, False), 0.0))
    west = 0.5 * (moved(diffusivity, 1, True) + diffusivity)
    east = 0.5 * (diffusivity + moved(diffusivity, 1, False))
    coef[0] = jnp.where(north_open, north, 0.0)
    coef[1] = jnp.where(south_open, south, 0.0)
    coef[2] = west
    coef[3] = east
    coef[4] = north + south + west + east

    def operate(field, span, use):
        sea = shared[1]
        for t in range(n_tm):
            masked = [[field[s, v] * sea for v in range(variables)] for s in range(n_tm)]
            centre = (diag[t] + coef[4])[:, :span]
            for v in range(variables):
                here = masked[t][v]
                mixed = centre * here[:, :span]
                for w in range(variables):
                    mixed = mixed + factors_ref[v * variables + w, :, :span] * masked[t][w][:, :span]
                for s in range(n_tm):
                    mixed = mixed + factors_ref[variables * variables + t * n_tm + s, :, :span] * masked[s][v][:, :span]
                spread = (
                    coef[0, :, :span] * moved(here[:, :span], 0, True)
                    + coef[1, :, :span] * moved(here[:, :span], 0, False)
                    + coef[2, :, :span] * moved(here, 1, True)[:, :span]
                    + coef[3, :, :span] * moved(here, 1, False)[:, :span]
                )
                use(t, v, sea[:, :span] * (mixed - spread) + (1.0 - sea[:, :span]) * field[t, v, :, :span])

    def sum_of(products):
        return jnp.sum(jnp.sum(products, axis=1, keepdims=True), axis=0, keepdims=True)

    fields = [(t, v) for t in range(n_tm) for v in range(variables)]
    none = jnp.zeros((height, cols), jnp.float32)
    bb, bw, ww, uu, ub, us, cross = [none] * 7
    for t, v in fields:
        start = sea * right[t, v]
        right[t, v] = start
        bb = bb + start[:, :cols] * start[:, :cols]

    def first_image(t, v, result):
        nonlocal bw, ww
        image[t, v] = result
        here = result[:, :cols]
        bw = bw + right[t, v, :, :cols] * here
        ww = ww + here * here

    operate(right, width, first_image)
    bb, ww = sum_of(bb), sum_of(ww)
    usable = (bb > 0.0) & (ww > 0.0)
    alpha = jnp.where(usable, jnp.sqrt(bb / jnp.where(usable, ww, 1.0)), 1.0)
    for t, v in fields:
        start = right[t, v]
        left = start - alpha * image[t, v]
        change[t, v] = left
        left, start = left[:, :cols], start[:, :cols]
        uu = uu + left * left
        ub = ub + left * start

    def second_image(t, v, result):
        nonlocal us, cross
        left, start = change[t, v, :, :cols], right[t, v, :, :cols]
        us = us + left * result
        cross = cross + (left * image[t, v, :, :cols] + start * result)
        image[t, v, :, cols:] = result

    operate(change, cols, second_image)
    own_rows = pl.ds(pl.multiple_of(lat * rows, rows), rows)
    for v in range(variables):
        own_ref[0, v] = right[tm, v, own_rows, :cols]
        own_ref[1, v] = image[tm, v, own_rows, :cols]
        own_ref[2, v] = change[tm, v, own_rows, :cols]
        own_ref[3, v] = image[tm, v, own_rows, cols:]
    for k, value in enumerate((alpha, bb, sum_of(bw), sum_of(uu), sum_of(ub), sum_of(us), sum_of(cross))):
        sums_ref[0, k : k + 1] = jnp.broadcast_to(value, (1, cols))
    sums_ref[0, 7:8] = jnp.zeros((1, cols), jnp.float32)


def update_kernel(own_ref, mine_ref, near_ref, far_ref, solution_ref, residual_ref):
    devices = [near_ref[k] for k in range(near_ref.shape[0])] + [far_ref[k] for k in range(far_ref.shape[0])]

    def over(values):
        return functools.reduce(jnp.add, values)

    def sums(device):
        return [device[k : k + 1] for k in range(7)]

    norm_start = over([sums(d)[1] for d in devices])
    step_first = norm_start / over([sums(d)[2] for d in devices])
    squares = []
    for d in devices:
        alpha, bb, bw, uu, ub, us, cross = sums(d)
        rho = step_first / alpha
        squares.append(rho * rho * uu + 2.0 * rho * (1.0 - rho) * ub + (1.0 - rho) * (1.0 - rho) * bb)
    norm_next = over(squares)
    share = norm_next / norm_start
    products = []
    for d in devices:
        alpha, bb, bw, uu, ub, us, cross = sums(d)
        rho = step_first / alpha
        kappa = 1.0 - rho + share
        products.append(rho * rho * us + rho * kappa * cross + kappa * kappa * bw)
    step_second = norm_next / over(products)
    rho = step_first / mine_ref[0, 0:1]
    kappa = 1.0 - rho + share
    for v in range(own_ref.shape[1]):
        start, image, left, left_image = (own_ref[k, v] for k in range(4))
        solution_ref[0, v, 0] = step_first * start + step_second * (rho * left + kappa * start)
        residual_ref[0, v, 0] = rho * left + (1.0 - rho) * start - step_second * (rho * left_image + kappa * image)


def bits(count):
    return [1 << k for k in range(count.bit_length() - 1)]


def swapped(x, axis, bit):
    return lax.ppermute(x, axis, [(i, i ^ bit) for i in range(lax.axis_size(axis))])


def gathered(x, axis, crossed=0):
    near, offsets = x[None], [0]
    for bit in reversed(bits(lax.axis_size(axis))[1:]):
        near = jnp.concatenate([near, swapped(near, axis, bit | crossed)], axis=0)
        offsets = offsets + [j + bit for j in offsets]
    return near, swapped(near, axis, 1), offsets


def per_device(class_ids, coef_table, land_mask, cross_cov, time_metric, obs_values, obs_weight, obs_cells, obs_count, block_owner):
    n_lat, n_lon, n_tm = (lax.axis_size(axis) for axis in ("lat", "lon", "tm"))
    rows, cols = class_ids.shape[1:]
    variables = obs_values.shape[1]
    stats = variables + 1
    vmem = pl.BlockSpec(memory_space=pltpu.VMEM)
    height = n_lat * rows
    half = jax.ShapeDtypeStruct((n_lon // 2, stats * n_lat + SIDES * height // cols, rows, cols), jnp.float32)
    values = obs_values.transpose(1, 0, 2)
    arguments = (block_owner[:, 0], obs_count, coef_table, cross_cov, time_metric, values, obs_weight, obs_cells, class_ids, land_mask)
    places = [pltpu.SMEM] * 5 + [pltpu.VMEM] * 5
    keep, send, planes, factors = pl.pallas_call(
        tile_kernel,
        out_shape=(
            half,
            half,
            jax.ShapeDtypeStruct((1, rows, cols), jnp.float32),
            jax.ShapeDtypeStruct((variables * variables + n_tm * n_tm, 1, 2 * cols), jnp.float32),
        ),
        in_specs=[pl.BlockSpec(memory_space=pltpu.HBM)] * INPUTS,
        out_specs=(vmem,) * 4,
        scratch_shapes=[
            pltpu.VMEM((n_lon, n_lat, stats, rows, cols), jnp.float32),
            pltpu.VMEM((n_lon, rows, SIDES * height), jnp.float32),
            *[place(x.shape, x.dtype) for place, x in zip(places, arguments)],
            pltpu.SemaphoreType.DMA((INPUTS,)),
        ],
        compiler_params=pltpu.CompilerParams(vmem_limit_bytes=32 * 1024 * 1024),
    )(*[pltpu.with_memory_space_constraint(x, pltpu.HBM) for x in arguments])

    partial = keep + swapped(send, "lon", 1)
    for bit in bits(n_lon)[1:]:
        partial = partial[0::2] + swapped(partial[1::2], "lon", bit)
    summed, lat_offsets = partial[0], [0]
    count = summed.shape[0]
    for bit in bits(n_lat):
        given = swapped(jnp.concatenate([summed, planes], axis=0), "lat", bit)
        summed = summed + given[:count]
        planes = jnp.concatenate([planes, given[count:]], axis=0)
        lat_offsets = lat_offsets + [i + bit for i in lat_offsets]
    strip = jnp.concatenate([summed, planes], axis=0)

    near, far, offsets = gathered(strip, "tm")
    field = pltpu.VMEM((n_tm, variables, height, 2 * cols), jnp.float32)
    plane = pltpu.VMEM((n_tm, height, 2 * cols), jnp.float32)
    own, sums = pl.pallas_call(
        functools.partial(strip_kernel, offsets, lat_offsets),
        out_shape=(
            jax.ShapeDtypeStruct((4, variables, rows, cols), jnp.float32),
            jax.ShapeDtypeStruct((1, rows, cols), jnp.float32),
        ),
        in_specs=[vmem] * 3,
        out_specs=(vmem, vmem),
        scratch_shapes=[field, field, field, plane, pltpu.VMEM((5, height, 2 * cols), jnp.float32), plane],
        compiler_params=pltpu.CompilerParams(vmem_limit_bytes=24 * 1024 * 1024),
    )(factors, near, far)

    near, far, _ = gathered(sums[0], "lon", 1)
    out = jax.ShapeDtypeStruct((1, variables, 1, rows, cols), jnp.float32)
    return pl.pallas_call(
        update_kernel,
        out_shape=(out, out),
        in_specs=[vmem] * 4,
        out_specs=(vmem, vmem),
        compiler_params=pltpu.CompilerParams(vmem_limit_bytes=8 * 1024 * 1024),
    )(own, sums, near, far)


def solution(mesh):
    in_specs = (
        P(None, "lat", "lon"),
        P(),
        P(None, "lat", "lon"),
        P(),
        P(),
        P(ALL, None, None),
        P(ALL, None),
        P(ALL, None),
        P(ALL),
        P(ALL, None),
    )
    out_specs = (P("tm", None, None, "lat", "lon"), P("tm", None, None, "lat", "lon"))
    return jax.shard_map(per_device, mesh=mesh, in_specs=in_specs, out_specs=out_specs, check_vma=False)
```
